32 devices in a mesh: dp: 8 (over z, core), seq: 4 (over y, x).
Axes of the slice: x: 2, y: 2, z: 4, core: 2. Of those that a mesh axis runs over, the one named last changes fastest.
Arguments:
- frames: bfloat16 [16, 1024, 1024], P('dp', 'seq'), may hold values from -6 to 6
- skip_in: bfloat16 [16, 1024, 1024], P('dp', 'seq'), may hold values from -6 to 6
- cond: bfloat16 [16, 1024, 1024], P('dp', 'seq'), may hold values from -6 to 6
- seg_ids: int32 [16, 1024], P('dp', 'seq'), may hold values from 0 to 2, as said below
- drop_flags: int32 [16, 3], P('dp'), may hold values 0 or 1
- flow_times: float32 [16, 3], P('dp'), may hold values from 0 to 1
- w_skip: bfloat16 [2048, 1024], P('dp', 'seq'), may hold values from -0.125 to 0.125
- w_qkv: bfloat16 [1024, 3072], P('dp', 'seq'), may hold values from -0.1875 to 0.1875
- w_out: bfloat16 [1024, 1024], P('seq', 'dp'), may hold values from -1.5 to 1.5
- w_up: bfloat16 [1024, 4096], P('dp', 'seq'), may hold values from -0.1875 to 0.1875
- w_down: bfloat16 [4096, 1024], P('seq', 'dp'), may hold values from -0.09375 to 0.09375
- w_mod: bfloat16 [1024, 6144], P('dp', 'seq'), may hold values from -0.375 to 0.375
- cotangent: bfloat16 [16, 1024, 1024], P('dp', 'seq'), may hold values from -6 to 6
Outputs:
- output: bfloat16 [16, 1024, 1024], P('dp', 'seq')
- grad_frames: bfloat16 [16, 1024, 1024], P('dp', 'seq')
- grad_skip: bfloat16 [16, 1024, 1024], P('dp', 'seq')
- grad_w_skip: float32 [2048, 1024], P('dp', 'seq')
- grad_w_qkv: float32 [1024, 3072], P('dp', 'seq')
- grad_w_out: float32 [1024, 1024], P('seq', 'dp')
- grad_w_up: float32 [1024, 4096], P('dp', 'seq')
- grad_w_down: float32 [4096, 1024], P('seq', 'dp')
- grad_w_mod: float32 [1024, 6144], P('dp', 'seq')
The draws below stay inside these ranges and needn't reach their ends.
Inputs may be any that keep to these rules, and one draw needn't show every extreme that they name: `seg_ids`: in each row the ids never fall; utterance 1 begins within the first 256 frames and ends within the last 256 frames; utterances 0 and 2 are never empty.
All inputs are finite; a program needn't handle non-finite values. No bound on the sum of `drop_flags` on one device may be relied on, other than what follows from the above.
Results may differ from the reference program's by a relative error of at most 0.023.
Values may be sent and summed in bfloat16 or wider, within the bound.
No kernel may reach another device: no remote copies, remote signals or barrier semaphores. Data moves between devices by JAX's collectives and lax.ppermute only.
A program may use at most 256 MiB of HBM per device.

```python
import math
import jax
import jax.numpy as jnp
from jax import lax

D = 1024
HEADS = 16
FF = 4096
SEGS = 3
FR_DEV = 256
ROWS = 16
LENGTH = 1024


def draw_seg_ids(key, part):
    key = jax.random.fold_in(key, 11)
    first_key, last_key = jax.random.split(key)
    start_frame = jax.random.randint(first_key, (ROWS, 1), FR_DEV // 2, FR_DEV)
    finish_frame = LENGTH - jax.random.randint(last_key, (ROWS, 1), FR_DEV // 2, FR_DEV)
    places = jnp.arange(LENGTH, dtype=jnp.int32)[None, :]
    return (places >= start_frame).astype(jnp.int32) + (places >= finish_frame).astype(jnp.int32)


def place_ends(entries, key, smallest, largest):
    index_at = [jax.random.randint(jax.random.fold_in(key, axis), (), 0, length) for axis, length in enumerate(entries.shape)]
    widest = entries.shape.index(max(entries.shape))
    neighbour = index_at[:widest] + [(index_at[widest] + 1) % entries.shape[widest]] + index_at[widest + 1:]
    return entries.at[tuple(index_at)].set(smallest).at[tuple(neighbour)].set(largest)


def steps_of(rng, dims, shards, smallest, high):
    def one(position, shards_of):
        steps = jax.random.uniform(jax.random.fold_in(jax.random.fold_in(rng, 6), position), (shards_of,), jnp.float32, smallest / len(shards), high / len(shards))
        return jnp.repeat(jnp.exp(steps), dims[position] // shards_of).reshape((-1,) + (1,) * (len(dims) - position - 1))

    level = one(*shards[0])
    for cut in shards[1:]:
        level = level * one(*cut)
    return level


def scatter_about(stream_key, dims, deviation, bound, cuts=(), held_as=jnp.bfloat16):
    drawn = jax.random.normal(stream_key, dims, jnp.float32) * deviation
    if len(cuts) > 0:
        drawn = steps_of(stream_key, dims, cuts, -0.22, 0.18) * drawn
    return jnp.clip(drawn, min=-bound, max=bound).astype(held_as)


def setup_inputs(seed: int = 0) -> dict:
    key_list = jax.random.split(jax.random.key(seed), 14)
    return {
        "frames": scatter_about(key_list[0], (ROWS, LENGTH, D), 1.0, 6.0, ((0, 8), (1, 4))),
        "skip_in": scatter_about(key_list[1], (ROWS, LENGTH, D), 1.0, 6.0, ((0, 8), (1, 4))),
        "cond": scatter_about(key_list[2], (ROWS, LENGTH, D), 1.0, 6.0, ((0, 8), (1, 4))),
        "seg_ids": draw_seg_ids(jax.random.fold_in(key_list[13], 71), 0),
        "drop_flags": place_ends((jax.random.randint(key_list[4], (ROWS, SEGS), 0, 4) < 1).astype(jnp.int32), jax.random.fold_in(key_list[4], 1), 0, 1),
        "flow_times": jnp.clip(1.0 * jax.random.uniform(key_list[5], (ROWS, SEGS), jnp.float32) ** steps_of(key_list[5], (ROWS, SEGS), ((0, 8),), -0.2, 0.2), 0.0, 1.0),
        "w_skip": scatter_about(key_list[6], (2 * D, D), (2 * D) ** -0.5, 0.125, ((0, 8), (1, 4))),
        "w_qkv": scatter_about(key_list[7], (D, 3 * D), D ** -0.5, 0.1875, ((0, 8), (1, 4))),
        "w_out": scatter_about(key_list[8], (D, D), (max(1, D * 16 // LENGTH)) ** -0.5, 1.5, ((0, 4), (1, 8))),
        "w_up": scatter_about(key_list[9], (D, FF), D ** -0.5, 0.1875, ((0, 8), (1, 4))),
        "w_down": scatter_about(key_list[10], (FF, D), FF ** -0.5, 0.09375, ((0, 4), (1, 8))),
        "w_mod": scatter_about(key_list[11], (D, 6 * D), (D // 4) ** -0.5, 0.375, ((0, 8), (1, 4))),
        "cotangent": scatter_about(key_list[12], (ROWS, LENGTH, D), 1.0, 6.0, ((0, 8), (1, 4))),
    }


EPSILON = 1e-06
MASKED = -1e+30
PRECISE = lax.Precision.HIGHEST

@jax.custom_vjp
def low(v):
    return lax.optimization_barrier(v.astype(jnp.bfloat16)).astype(jnp.float32)

@jax.custom_vjp
def low_back(v):
    return v

def low_keep(v):
    return (low(v), None)

def low_pass(kept, grad):
    return (grad,)

def back_keep(v):
    return (v, None)

def back_low(kept, grad):
    return (low(grad),)
low.defvjp(low_keep, low_pass)
low_back.defvjp(back_keep, back_low)

def norm_mod(hidden, offset, factor):
    centre = hidden - lax.optimization_barrier(jnp.mean(hidden, -1, keepdims=True))
    variance = lax.optimization_barrier(jnp.mean(centre * centre, -1, keepdims=True))
    return centre * lax.rsqrt(variance + EPSILON) * (1.0 + factor) + offset

def rope_tables(positions, head_dim):
    half_dim = head_dim // 2
    frequency = jnp.exp(jnp.arange(half_dim, dtype=jnp.float32) * (-2.0 * math.log(10000.0) / head_dim))
    angles = positions.astype(jnp.float32)[:, None] * frequency[None, :]
    return (jnp.cos(angles), jnp.sin(angles))

def rotate(values, cosine, sine_table):
    half_dim = values.shape[-1] // 2
    lower_half = values[..., :half_dim]
    upper_half = values[..., half_dim:]
    cos_part = cosine[:, None, :]
    sin_part = sine_table[:, None, :]
    return jnp.concatenate([lower_half * cos_part - upper_half * sin_part, upper_half * cos_part + lower_half * sin_part], -1)

def time_embed(flow_values, model_width):
    half_dim = model_width // 2
    frequency = jnp.exp(jnp.arange(half_dim, dtype=jnp.float32) * (-math.log(10000.0) / half_dim))
    angles = 1000.0 * flow_values[..., None] * frequency
    return jnp.concatenate([jnp.sin(angles), jnp.cos(angles)], -1)

def attend_block(query_block, seg_block, key_rows, value_rows, seg_row):
    head_dim = key_rows.shape[-1]
    scores = jnp.einsum('qhd,khd->hqk', query_block, key_rows, precision=PRECISE) * head_dim ** (-0.5)
    scores = low_back(scores)
    allowed = (seg_block[:, None] == seg_row[None, :])[None]
    scores = jnp.where(allowed, scores, MASKED)
    weights_p = low(jax.nn.softmax(scores, axis=-1))
    return jnp.einsum('hqk,khd->qhd', weights_p, value_rows, precision=PRECISE)

def row_forward(weights, frames_row, skip_row, cond_row, seg_row, drop_row, time_row, cond_scale):
    w_skip, w_qkv, w_out, w_up, w_down, w_mod = weights
    length, model_width = frames_row.shape
    head_dim = model_width // HEADS
    seg_count = time_row.shape[0]
    onehot = (seg_row[:, None] == jnp.arange(seg_count, dtype=jnp.int32)[None, :]).astype(jnp.float32)
    activity = low(jax.nn.silu(time_embed(time_row, model_width)))
    modulation = jnp.dot(activity, w_mod, precision=PRECISE)
    per_frame = jnp.dot(onehot, modulation, precision=PRECISE)
    shift_one, scale_one, gate_one, shift_two, scale_two, gate_two = jnp.split(per_frame, 6, axis=1)
    keep_frame = 1.0 - lax.optimization_barrier(jnp.sum(onehot * drop_row.astype(jnp.float32)[None, :], -1))
    joined = jnp.concatenate([frames_row, skip_row], -1)
    hidden = low_back(jnp.dot(joined, w_skip, precision=PRECISE)) + (keep_frame * cond_scale)[:, None] * cond_row
    normed = low(norm_mod(hidden, shift_one, scale_one))
    projected = low_back(jnp.dot(normed, w_qkv, precision=PRECISE))
    proj_heads = projected.reshape(length, HEADS, 3, head_dim)
    cosine, sine_table = rope_tables(jnp.arange(length, dtype=jnp.int32), head_dim)
    queries = low(low_back(rotate(proj_heads[:, :, 0], cosine, sine_table)))
    key_rows = low(low_back(rotate(proj_heads[:, :, 1], cosine, sine_table)))
    value_rows = low(low_back(proj_heads[:, :, 2]))
    block_rows = min(512, length)
    blocks = length // block_rows

    def one_block(inputs):
        return attend_block(inputs[0], inputs[1], key_rows, value_rows, seg_row)
    attended = lax.map(jax.checkpoint(one_block), (queries.reshape(blocks, block_rows, HEADS, head_dim), seg_row.reshape(blocks, block_rows)))
    attended = low(low_back(attended.reshape(length, model_width)))
    branch = low_back(jnp.dot(attended, w_out, precision=PRECISE))
    middle = hidden + gate_one * branch
    normed_two = low(norm_mod(middle, shift_two, scale_two))
    pre_act = low_back(jnp.dot(normed_two, w_up, precision=PRECISE))
    activated = low(jax.nn.gelu(pre_act, approximate=True))
    fed = low_back(jnp.dot(activated, w_down, precision=PRECISE))
    return middle + gate_two * fed

def reference(frames, skip_in, cond, seg_ids, drop_flags, flow_times, w_skip, w_qkv, w_out, w_up, w_down, w_mod, cotangent):
    params = tuple((weight.astype(jnp.float32) for weight in (w_skip, w_qkv, w_out, w_up, w_down, w_mod)))
    slots = ROWS * SEGS
    dropped = jnp.sum(drop_flags).astype(jnp.float32)
    cond_scale = slots / jnp.maximum(slots - dropped, 1.0)

    def row_step(grad_total, row_data):
        frames_row, skip_row, cond_row, seg_row, drop_row, time_row, cot_row = row_data

        def forward(weights, frames_value, skip_value):
            return row_forward(weights, frames_value, skip_value, cond_row.astype(jnp.float32), seg_row, drop_row, time_row, cond_scale)
        out_row, pullback = jax.vjp(forward, params, frames_row.astype(jnp.float32), skip_row.astype(jnp.float32))
        grad_params, grad_frames_row, grad_skip_row = pullback(cot_row.astype(jnp.float32))
        grad_total = tuple((left + right for left, right in zip(grad_total, grad_params)))
        return (grad_total, (out_row.astype(jnp.bfloat16), grad_frames_row.astype(jnp.bfloat16), grad_skip_row.astype(jnp.bfloat16)))
    zeros_start = tuple((jnp.zeros(weight.shape, jnp.float32) for weight in params))
    grad_total, outputs = lax.scan(row_step, zeros_start, (frames, skip_in, cond, seg_ids, drop_flags, flow_times, cotangent))
    output, grad_frames, grad_skip = outputs
    return (output, grad_frames, grad_skip, grad_total[0], grad_total[1], grad_total[2], grad_total[3], grad_total[4], grad_total[5])
```

```python
import functools
import math

import jax
import jax.numpy as jnp
from jax import lax
from jax.experimental import pallas as pl
from jax.experimental.pallas import tpu as pltpu
from jax.sharding import PartitionSpec as P

HEADS = 16
CORES = 2
EPSILON = 1e-06
MASKED = -1e30
VMEM_LIMIT = 60 * 1024 * 1024
F32 = jnp.float32
BF16 = jnp.bfloat16
NT = (((1,), (1,)), ((), ()))
TN = (((0,), (0,)), ((), ()))


def dot(left, right):
    return jnp.dot(left, right, preferred_element_type=F32)


def against(left, right):
    return lax.dot_general(left, right, NT, preferred_element_type=F32)


def over_rows(left, right):
    return lax.dot_general(left, right, TN, preferred_element_type=F32)


def swap(values, axis, mask):
    return lax.ppermute(values, axis, [(i, i ^ mask) for i in range(lax.axis_size(axis))])


def chip_masks():
    return [CORES * k for k in range(1, lax.axis_size("dp") // CORES)]


def seq_halves():
    count = lax.axis_size("seq")
    fast = 1
    while fast * fast < count:
        fast *= 2
    slow = count // fast
    return [list(range(1, fast)), [fast * k for k in range(1, slow)]]


def gather_steps(shard, steps):
    held = shard
    for axis, masks in steps:
        held = jnp.stack([held] + [swap(held, axis, mask) for mask in masks])
    return held


def assemble_kernel(steps, rows, columns, relative, place_ref, mine_ref, other_ref, out_ref, sems):
    lead = mine_ref.shape[:-2]
    copies = []
    for flat in range(math.prod(lead)):
        index, rest = [], flat
        for size in reversed(lead):
            index.insert(0, rest % size)
            rest //= size
        dp_mask, seq_mask = 0, 0
        for position, (axis, masks) in zip(index, reversed(steps)):
            mask = ([0] + masks)[position]
            if axis == "dp":
                dp_mask ^= mask
            else:
                seq_mask ^= mask
        for core, source in ((0, mine_ref), (1, other_ref)):
            row = pl.multiple_of((place_ref[0] ^ (dp_mask ^ core)) * rows, rows)
            if relative == "blocks":
                target = out_ref.at[seq_mask, pl.ds(row, rows), :]
            elif relative == "columns":
                target = out_ref.at[pl.ds(row, rows), pl.ds(seq_mask * columns, columns)]
            elif len(steps) == 1:
                target = out_ref.at[pl.ds(row, rows), :]
            else:
                column = pl.multiple_of((place_ref[1] ^ seq_mask) * columns, columns)
                target = out_ref.at[pl.ds(row, rows), pl.ds(column, columns)]
            copies.append(pltpu.make_async_copy(source.at[tuple(index)], target, sems.at[len(copies)]))
    for copy in copies:
        copy.start()
    for copy in copies:
        copy.wait()


def fetch(shard, place, seq_order, relative):
    rows, columns = shard.shape
    dp_size, seq_size = lax.axis_size("dp"), lax.axis_size("seq")
    seqs = 1 if seq_order is None else seq_size
    if columns % 128 and seqs > 1:
        held = lax.all_gather(lax.all_gather(shard, "dp", axis=0, tiled=True), "seq", axis=0)
        if relative:
            held = jnp.take(held, jnp.arange(seqs) ^ place[1], axis=0)
        if relative == "blocks":
            return held
        return jnp.moveaxis(held, 0, 1).reshape(dp_size * rows, seqs * columns)
    steps = [("dp", chip_masks())]
    if seqs > 1:
        halves = seq_halves()
        steps += [("seq", halves[k]) for k in seq_order]
    mine = gather_steps(shard, steps)
    other = swap(mine, "dp", 1)
    if relative == "blocks":
        shape = (seqs, dp_size * rows, columns)
    else:
        shape = (dp_size * rows, seqs * columns)
    return pl.pallas_call(
        functools.partial(assemble_kernel, steps, rows, columns, relative),
        out_shape=jax.ShapeDtypeStruct(shape, shard.dtype),
        in_specs=[
            pl.BlockSpec(memory_space=pltpu.SMEM),
            pl.BlockSpec(memory_space=pl.ANY),
            pl.BlockSpec(memory_space=pl.ANY),
        ],
        out_specs=pl.BlockSpec(memory_space=pltpu.VMEM),
        scratch_shapes=[pltpu.SemaphoreType.DMA((dp_size * seqs,))],
        compiler_params=pltpu.CompilerParams(vmem_limit_bytes=VMEM_LIMIT),
        cost_estimate=pl.CostEstimate(flops=0, bytes_accessed=4 * dp_size * seqs * rows * columns, transcendentals=0),
        name="assemble",
    )(place, mine, other)


def pick(values, index, axis):
    return lax.dynamic_index_in_dim(values, index, axis, keepdims=False)


def reduce_weight(blocks, rows, dp):
    chips = lax.axis_size("dp") // CORES
    core, chip = dp % CORES, dp // CORES
    columns = blocks[0].shape[-1]
    shaped = [block.reshape(chips, CORES, rows, columns) for block in blocks]
    give = jnp.stack([pick(block, 1 - core, 1).astype(BF16) for block in shaped])
    got = swap(give, "dp", 1)
    held = [pick(block, core, 1).astype(F32) + got[m].astype(F32) for m, block in enumerate(shaped)]
    if len(held) > 1:
        fast, slow = seq_halves()
        sent = {}
        for mask in fast:
            sent[mask] = swap(jnp.stack([held[s ^ mask] for s in [0] + slow]).astype(BF16), "seq", mask)
        kept = []
        for position, base in enumerate([0] + slow):
            total = held[base]
            for mask in fast:
                total = total + sent[mask][position].astype(F32)
            kept.append(total)
        total = kept[0]
        for position, mask in enumerate(slow):
            total = total + swap(kept[1 + position].astype(BF16), "seq", mask).astype(F32)
    else:
        total = held[0]
    result = pick(total, chip, 0)
    for mask in chip_masks():
        result = result + swap(pick(total, chip ^ (mask // CORES), 0).astype(BF16), "dp", mask).astype(F32)
    return result


def qkv_kernel(width, scale, x_ref, w_ref, cos_ref, sin_ref, *rest):
    out_ref = rest[-1]
    half = width // 2
    projected = dot(x_ref[0], w_ref[...])
    cosine, sine = cos_ref[0], sin_ref[0]
    for part, factor in ((0, scale), (1, 1.0)):
        low = projected[:, part * width : part * width + half]
        high = projected[:, part * width + half : (part + 1) * width]
        out_ref[0, 0, :, part * width : part * width + half] = ((low * cosine - high * sine) * factor).astype(BF16)
        out_ref[0, 0, :, part * width + half : (part + 1) * width] = ((high * cosine + low * sine) * factor).astype(BF16)
    out_ref[0, 0, :, 2 * width :] = projected[:, 2 * width :].astype(BF16)


def project_piece(piece, normed, weights, cos_table, sin_table, held, scale):
    rows, frames, model = normed.shape
    pieces = cos_table.shape[0]
    width = weights.shape[1] // 3
    in_specs = [
        pl.BlockSpec((1, frames, model), lambda r: (r, 0, 0)),
        pl.BlockSpec((model, 3 * width), lambda r: (0, 0)),
        pl.BlockSpec((1, frames, width // 2), lambda r: (piece, 0, 0)),
        pl.BlockSpec((1, frames, width // 2), lambda r: (piece, 0, 0)),
    ]
    arrays = [normed, weights, cos_table, sin_table]
    aliases = {}
    if held is not None:
        in_specs.append(pl.BlockSpec(memory_space=pl.ANY))
        arrays.append(held)
        aliases = {4: 0}
    return pl.pallas_call(
        functools.partial(qkv_kernel, width, scale),
        grid=(rows,),
        out_shape=jax.ShapeDtypeStruct((pieces, rows, frames, 3 * width), BF16),
        in_specs=in_specs,
        out_specs=pl.BlockSpec((1, 1, frames, 3 * width), lambda r: (piece, r, 0, 0)),
        input_output_aliases=aliases,
        compiler_params=pltpu.CompilerParams(vmem_limit_bytes=VMEM_LIMIT),
        cost_estimate=pl.CostEstimate(
            flops=2 * rows * frames * model * 3 * width, bytes_accessed=5 * rows * frames * model, transcendentals=0
        ),
        name="project",
    )(*arrays)


def head_lanes(shape, heads, width, split):
    lane = lax.broadcasted_iota(jnp.int32, shape, 1)
    size = width // heads
    if split:
        return (lane % (width // 2)) // (size // 2)
    return lane // size


def attend_kernel(heads, width, qkv_ref, seg_col_ref, seg_row_ref, out_ref, lse_ref, vt_ref, ot_ref):
    pieces, _, frames, _ = qkv_ref.shape
    length = pieces * frames
    step = pl.program_id(1)
    size = width // heads
    keys = qkv_ref[:, 0, :, width : 2 * width].reshape(length, width)

    @pl.when(step == 0)
    def _():
        vt_ref[...] = qkv_ref[:, 0, :, 2 * width :].reshape(length, width).T

    queries = qkv_ref[step, 0, :, :width]
    owner = head_lanes((frames, width), heads, width, True)
    allowed = seg_col_ref[0] == seg_row_ref[0, 0]
    for head in range(heads):
        masked = jnp.where(owner == head, queries, jnp.zeros_like(queries))
        scores = jnp.where(allowed, against(keys, masked), MASKED)
        highest = jnp.max(scores, 0, keepdims=True)
        raised = jnp.exp(scores - highest)
        total = jnp.sum(raised, 0, keepdims=True)
        lse_ref[0, 0, head : head + 1, :] = highest + jnp.log(total)
        result = dot(vt_ref[head * size : (head + 1) * size, :], raised.astype(BF16))
        ot_ref[head * size : (head + 1) * size, :] = result / total
    out_ref[0, 0] = ot_ref[...].T.astype(BF16)


def attend(qkv, seg_col, seg_row, heads):
    pieces, rows, frames, triple = qkv.shape
    width = triple // 3
    length = pieces * frames
    return pl.pallas_call(
        functools.partial(attend_kernel, heads, width),
        grid=(rows, pieces),
        out_shape=(
            jax.ShapeDtypeStruct((pieces, rows, frames, width), BF16),
            jax.ShapeDtypeStruct((rows, pieces, heads, frames), F32),
        ),
        in_specs=[
            pl.BlockSpec((pieces, 1, frames, triple), lambda r, s: (0, r, 0, 0)),
            pl.BlockSpec((1, length, 1), lambda r, s: (r, 0, 0)),
            pl.BlockSpec((1, 1, 1, frames), lambda r, s: (r, s, 0, 0)),
        ],
        out_specs=(
            pl.BlockSpec((1, 1, frames, width), lambda r, s: (s, r, 0, 0)),
            pl.BlockSpec((1, 1, heads, frames), lambda r, s: (r, s, 0, 0)),
        ),
        scratch_shapes=[pltpu.VMEM((width, length), BF16), pltpu.VMEM((width, frames), F32)],
        compiler_params=pltpu.CompilerParams(vmem_limit_bytes=VMEM_LIMIT),
        cost_estimate=pl.CostEstimate(
            flops=4 * rows * length * length * 256 * heads,
            bytes_accessed=8 * rows * length * width,
            transcendentals=rows * heads * length * length,
        ),
        name="attend",
    )(qkv, seg_col, seg_row)


def attend_back_kernel(
    heads, width, scale, qkv_ref, seg_col_ref, seg_row_ref, out_ref, lse_ref, grad_ref, cos_ref, sin_ref,
    result_ref, kt_ref, dk_ref, dv_ref, dqt_ref,
):
    pieces, _, frames, _ = qkv_ref.shape
    length = pieces * frames
    step = pl.program_id(1)
    size, half = width // heads, width // 2
    keys = qkv_ref[:, 0, :, width : 2 * width].reshape(length, width)
    values = qkv_ref[:, 0, :, 2 * width :].reshape(length, width)

    @pl.when(step == 0)
    def _():
        kt_ref[...] = keys.T
        dk_ref[...] = jnp.zeros_like(dk_ref)
        dv_ref[...] = jnp.zeros_like(dv_ref)

    queries = qkv_ref[step, 0, :, :width]
    grad = grad_ref[0, 0]
    query_owner = head_lanes((frames, width), heads, width, True)
    value_owner = head_lanes((frames, width), heads, width, False)
    allowed = seg_col_ref[0] == seg_row_ref[0, 0]
    product = grad.astype(F32) * out_ref[0, 0].astype(F32)
    picker = lax.broadcasted_iota(jnp.int32, (8, width), 1) // size == lax.broadcasted_iota(jnp.int32, (8, width), 0)
    inner = lax.dot_general(
        picker.astype(F32), product, NT, precision=lax.Precision.HIGHEST, preferred_element_type=F32
    )
    for head in range(heads):
        masked = jnp.where(query_owner == head, queries, jnp.zeros_like(queries))
        masked_grad = jnp.where(value_owner == head, grad, jnp.zeros_like(grad))
        scores = against(keys, masked)
        weights = jnp.where(allowed, jnp.exp(scores - lse_ref[0, 0, head : head + 1, :]), 0.0)
        grad_weights = against(values, masked_grad)
        grad_scores = (weights * (grad_weights - inner[head : head + 1, :])).astype(BF16)
        dv_ref[...] += dot(weights.astype(BF16), masked_grad)
        dk_ref[...] += dot(grad_scores, masked)
        low, high = head * size // 2, half + head * size // 2
        head_keys = jnp.concatenate([kt_ref[low : low + size // 2, :], kt_ref[high : high + size // 2, :]], 0)
        part = dot(head_keys, grad_scores)
        dqt_ref[low : low + size // 2, :] = part[: size // 2]
        dqt_ref[high : high + size // 2, :] = part[size // 2 :]

    def unrotate(values, cosine, sine):
        low, high = values[:, :half], values[:, half:]
        return (low * cosine + high * sine).astype(BF16), (high * cosine - low * sine).astype(BF16)

    low, high = unrotate(dqt_ref[...].T * scale, cos_ref[step], sin_ref[step])
    result_ref[step, 0, :, :half] = low
    result_ref[step, 0, :, half:width] = high

    @pl.when(step == pieces - 1)
    def _():
        for piece in range(pieces):
            span = slice(piece * frames, (piece + 1) * frames)
            low, high = unrotate(dk_ref[span, :], cos_ref[piece], sin_ref[piece])
            result_ref[piece, 0, :, width : width + half] = low
            result_ref[piece, 0, :, width + half : 2 * width] = high
            result_ref[piece, 0, :, 2 * width :] = dv_ref[span, :].astype(BF16)


def attend_back(qkv, seg_col, seg_row, out, lse, grad, cos_table, sin_table, heads, scale):
    pieces, rows, frames, triple = qkv.shape
    width = triple // 3
    length = pieces * frames
    whole = pl.BlockSpec((pieces, 1, frames, triple), lambda r, s: (0, r, 0, 0))
    table = pl.BlockSpec((pieces, frames, width // 2), lambda r, s: (0, 0, 0))
    block = pl.BlockSpec((1, 1, frames, width), lambda r, s: (s, r, 0, 0))
    return pl.pallas_call(
        functools.partial(attend_back_kernel, heads, width, scale),
        grid=(rows, pieces),
        out_shape=jax.ShapeDtypeStruct(qkv.shape, BF16),
        in_specs=[
            whole,
            pl.BlockSpec((1, length, 1), lambda r, s: (r, 0, 0)),
            pl.BlockSpec((1, 1, 1, frames), lambda r, s: (r, s, 0, 0)),
            block,
            pl.BlockSpec((1, 1, heads, frames), lambda r, s: (r, s, 0, 0)),
            block,
            table,
            table,
        ],
        out_specs=whole,
        scratch_shapes=[
            pltpu.VMEM((width, length), BF16),
            pltpu.VMEM((length, width), F32),
            pltpu.VMEM((length, width), F32),
            pltpu.VMEM((width, frames), F32),
        ],
        compiler_params=pltpu.CompilerParams(vmem_limit_bytes=VMEM_LIMIT),
        cost_estimate=pl.CostEstimate(
            flops=10 * rows * length * length * 256 * heads,
            bytes_accessed=16 * rows * length * width,
            transcendentals=rows * heads * length * length,
        ),
        name="attend_back",
    )(qkv, seg_col, seg_row, out, lse, grad, cos_table, sin_table)


def mlp_kernel(normed_ref, grad_ref, up_ref, down_ref, fed_ref, gn_ref, gup_ref, gdown_ref, nt_ref, gt_ref):
    @pl.when(pl.program_id(0) == 0)
    def _():
        nt_ref[...] = normed_ref[...].T
        gt_ref[...] = grad_ref[...].T
        fed_ref[...] = jnp.zeros_like(fed_ref)
        gn_ref[...] = jnp.zeros_like(gn_ref)

    up, down = up_ref[0], down_ref[0]
    before = dot(normed_ref[...], up)
    square = before * before
    factor = math.sqrt(2.0 / math.pi)
    bent = jnp.tanh(factor * (before + 0.044715 * (square * before)))
    activated = (0.5 * before * (1.0 + bent)).astype(BF16)
    slope = 0.5 * (1.0 + bent) + 0.5 * before * (1.0 - bent * bent) * (factor * (1.0 + 3 * 0.044715 * square))
    grad_before = (dot(grad_ref[...], down) * slope).astype(BF16)
    fed_ref[...] += against(activated, down)
    gn_ref[...] += against(grad_before, up)
    gup_ref[0] = dot(nt_ref[...], grad_before).astype(BF16)
    gdown_ref[0] = dot(gt_ref[...], activated).astype(BF16)


def mlp(normed, grad, up, down):
    tokens, model = normed.shape
    blocks, _, columns = up.shape
    chunk = min(512, columns)
    per_block = columns // chunk
    whole = pl.BlockSpec((tokens, model), lambda i: (0, 0))
    weight = pl.BlockSpec((1, model, chunk), lambda i: (i // per_block, 0, i % per_block))
    return pl.pallas_call(
        mlp_kernel,
        grid=(blocks * per_block,),
        out_shape=(
            jax.ShapeDtypeStruct((tokens, model), F32),
            jax.ShapeDtypeStruct((tokens, model), F32),
            jax.ShapeDtypeStruct(up.shape, BF16),
            jax.ShapeDtypeStruct(up.shape, BF16),
        ),
        in_specs=[whole, whole, weight, weight],
        out_specs=(whole, whole, weight, weight),
        scratch_shapes=[pltpu.VMEM((model, tokens), BF16), pltpu.VMEM((model, tokens), BF16)],
        compiler_params=pltpu.CompilerParams(vmem_limit_bytes=VMEM_LIMIT),
        cost_estimate=pl.CostEstimate(
            flops=12 * tokens * model * blocks * columns,
            bytes_accessed=8 * model * blocks * columns + 12 * tokens * model,
            transcendentals=tokens * blocks * columns,
        ),
        name="mlp",
    )(normed, grad, up, down)


def standardize(values):
    centre = values - jnp.mean(values, -1, keepdims=True)
    inverse = lax.rsqrt(jnp.mean(centre * centre, -1, keepdims=True) + EPSILON)
    return centre * inverse, inverse


def standardize_back(grad, standard, inverse):
    return inverse * (
        grad - jnp.mean(grad, -1, keepdims=True) - standard * jnp.mean(grad * standard, -1, keepdims=True)
    )


def time_embed(flow_values, model_width):
    half_dim = model_width // 2
    frequency = jnp.exp(jnp.arange(half_dim, dtype=F32) * (-math.log(10000.0) / half_dim))
    angles = 1000.0 * flow_values[..., None] * frequency
    return jnp.concatenate([jnp.sin(angles), jnp.cos(angles)], -1)


def body(
    frames, skip_in, cond, seg_ids, drop_flags, flow_times, w_skip, w_qkv, w_out, w_up, w_down, w_mod, cotangent
):
    row_count, frame_count, model = frames.shape
    seq_size, dp_size = lax.axis_size("seq"), lax.axis_size("dp")
    chips = dp_size // CORES
    dp, seq = lax.axis_index("dp"), lax.axis_index("seq")
    place = jnp.stack([dp, seq]).astype(jnp.int32)
    head_dim = model // HEADS
    heads = HEADS // seq_size
    width = heads * head_dim
    half = head_dim // 2
    scale = head_dim ** (-0.5)
    length = frame_count * seq_size
    tokens = row_count * frame_count
    segs = drop_flags.shape[1]
    frame_shape = (row_count, frame_count, model)
    partners = range(1, seq_size)

    by_head = w_qkv.reshape(w_qkv.shape[0], heads, 3, 2, half)
    qkv_shard = jnp.concatenate(
        [
            by_head[:, :, 0].swapaxes(1, 2).reshape(-1, width),
            by_head[:, :, 1].swapaxes(1, 2).reshape(-1, width),
            by_head[:, :, 2].reshape(-1, width),
        ],
        1,
    )

    small = jnp.concatenate([flow_times, drop_flags.astype(F32)], 1)
    small = gather_steps(small, [("dp", chip_masks()), ("dp", [1])])
    dropped = jnp.sum(small[..., segs:])
    slots = float(row_count * segs * dp_size)
    cond_scale = slots / jnp.maximum(slots - dropped, 1.0)
    utterances = row_count * segs
    activity = jax.nn.silu(time_embed(small[..., :segs], model)).astype(BF16).reshape(dp_size * utterances, model)
    mod_rows, mod_columns = w_mod.shape
    activity = lax.dynamic_slice_in_dim(activity, dp * mod_rows, mod_rows, 1)

    skip_full = fetch(w_skip, place, [1, 0], "")
    partial = dot(activity, w_mod).reshape(CORES, chips, utterances, mod_columns)
    partial = partial[0] + swap(partial[1], "dp", 1)
    modulation = partial[0]
    for mask in chip_masks():
        modulation = modulation + swap(partial[mask // CORES], "dp", mask)
    modulation = jnp.stack([modulation] + [swap(modulation, "seq", mask) for mask in partners])
    modulation = jnp.take(modulation, jnp.arange(seq_size) ^ seq, axis=0)
    modulation = modulation.swapaxes(0, 1).reshape(row_count, segs, 6, model)

    onehot = (seg_ids[:, :, None] == jnp.arange(segs, dtype=jnp.int32)).astype(F32)

    def spread(part):
        result = onehot[:, :, 0, None] * modulation[:, 0, None, part, :]
        for position in range(1, segs):
            result = result + onehot[:, :, position, None] * modulation[:, position, None, part, :]
        return result.reshape(tokens, model)

    shift_one, scale_one, gate_one, shift_two, scale_two, gate_two = (spread(part) for part in range(6))
    keep_frame = (1.0 - jnp.sum(onehot * drop_flags.astype(F32)[:, None, :], -1)).reshape(tokens, 1)

    qkv_full = fetch(qkv_shard, place, None, "")
    out_full = fetch(w_out.T, place, [0, 1], "columns")
    up_full = fetch(w_up, place, [1, 0], "blocks")
    down_full = fetch(w_down.T, place, [0, 1], "blocks")

    joined = jnp.concatenate([frames, skip_in], -1).reshape(tokens, 2 * model)
    hidden = dot(joined, skip_full) + keep_frame * cond_scale * cond.reshape(tokens, model).astype(F32)
    standard_one, inverse_one = standardize(hidden)
    normed = (standard_one * (1.0 + scale_one) + shift_one).astype(BF16).reshape(frame_shape)

    segments = jnp.stack([seg_ids] + [swap(seg_ids, "seq", mask) for mask in partners])
    seg_row = segments.swapaxes(0, 1).reshape(row_count, seq_size, 1, frame_count)
    seg_col = segments.swapaxes(0, 1).reshape(row_count, length, 1)
    positions = (jnp.arange(seq_size) ^ seq)[:, None] * frame_count + jnp.arange(frame_count)
    frequency = jnp.exp(jnp.arange(half, dtype=F32) * (-2.0 * math.log(10000.0) / head_dim))
    angles = positions.astype(F32)[..., None] * frequency
    cos_table = jnp.tile(jnp.cos(angles), (1, 1, heads))
    sin_table = jnp.tile(jnp.sin(angles), (1, 1, heads))

    pieces = [normed] + [swap(normed, "seq", mask) for mask in partners]
    qkv = None
    for position, piece in enumerate(pieces):
        qkv = project_piece(position, piece, qkv_full, cos_table, sin_table, qkv, scale)
    attended, lse = attend(qkv, seg_col, seg_row, heads)
    blocks = [attended[0]] + [swap(attended[mask], "seq", mask) for mask in partners]
    attn = jnp.concatenate(blocks, -1).reshape(tokens, model)

    branch = against(attn, out_full)
    middle = hidden + gate_one * branch
    standard_two, inverse_two = standardize(middle)
    normed_two = (standard_two * (1.0 + scale_two) + shift_two).astype(BF16)
    grad_out = cotangent.reshape(tokens, model).astype(F32)
    grad_fed = (gate_two * grad_out).astype(BF16)
    fed, grad_norm_two, grad_up, grad_down = mlp(normed_two, grad_fed, up_full, down_full)
    output = (middle + gate_two * fed).astype(BF16).reshape(frame_shape)

    rows = w_up.shape[0]
    sum_down = reduce_weight([grad_down[m] for m in range(seq_size)], rows, dp).T
    sum_up = reduce_weight([grad_up[m] for m in range(seq_size)], rows, dp)

    grad_middle = grad_out + standardize_back(grad_norm_two * (1.0 + scale_two), standard_two, inverse_two)
    grad_branch = (gate_one * grad_middle).astype(BF16)
    grad_attn = dot(grad_branch, out_full).astype(BF16).reshape(row_count, frame_count, seq_size, width)
    grad_blocks = [grad_attn[:, :, m] for m in range(seq_size)]
    grad_heads = jnp.stack([grad_blocks[0]] + [swap(grad_blocks[m], "seq", m) for m in partners])
    grad_w_out = over_rows(grad_branch, attn).astype(BF16)
    sum_out = reduce_weight([grad_w_out[:, m * width : (m + 1) * width] for m in range(seq_size)], rows, dp).T

    grad_qkv = attend_back(qkv, seg_col, seg_row, attended, lse, grad_heads, cos_table, sin_table, heads, scale)
    flat_grad = grad_qkv.reshape(seq_size, tokens, 3 * width)
    grad_normed = None
    for mask in list(partners) + [0]:
        part = against(flat_grad[mask], qkv_full)
        if mask:
            part = swap(part.astype(BF16), "seq", mask).astype(F32)
        grad_normed = part if grad_normed is None else grad_normed + part
    grad_w_qkv = over_rows(
        jnp.concatenate([piece.reshape(tokens, model) for piece in pieces]),
        flat_grad.reshape(seq_size * tokens, 3 * width),
    ).astype(BF16)
    sum_qkv = reduce_weight([grad_w_qkv], rows, dp)
    sum_qkv = jnp.stack(
        [
            sum_qkv[:, :width].reshape(rows, 2, heads, half).swapaxes(1, 2).reshape(rows, heads, head_dim),
            sum_qkv[:, width : 2 * width].reshape(rows, 2, heads, half).swapaxes(1, 2).reshape(rows, heads, head_dim),
            sum_qkv[:, 2 * width :].reshape(rows, heads, head_dim),
        ],
        2,
    ).reshape(rows, 3 * width)

    grad_hidden = (
        grad_middle + standardize_back(grad_normed * (1.0 + scale_one), standard_one, inverse_one)
    ).astype(BF16)
    grad_joined = against(grad_hidden, skip_full).astype(BF16)
    grad_frames = grad_joined[:, :model].reshape(frame_shape)
    grad_skip = grad_joined[:, model:].reshape(frame_shape)
    grad_columns = jnp.concatenate(
        [lax.dynamic_slice_in_dim(grad_hidden, (seq ^ m) * width, width, 1) for m in range(seq_size)], 1
    )
    grad_w_skip = over_rows(joined, grad_columns).astype(BF16)
    sum_skip = reduce_weight(
        [grad_w_skip[:, m * width : (m + 1) * width] for m in range(seq_size)], w_skip.shape[0], dp
    )

    def per_utterance(values):
        return jnp.einsum(
            "rfs,rfc->rsc", onehot, values.reshape(frame_shape), precision=lax.Precision.HIGHEST
        ).reshape(utterances, model)

    grad_modulation = jnp.concatenate(
        [
            per_utterance(grad_normed),
            per_utterance(grad_normed * standard_one),
            per_utterance(grad_middle * branch),
            per_utterance(grad_norm_two),
            per_utterance(grad_norm_two * standard_two),
            per_utterance(grad_out * fed),
        ],
        1,
    )
    own = lax.dynamic_slice_in_dim(grad_modulation, seq * mod_columns, mod_columns, 1)
    for mask in partners:
        own = own + swap(
            lax.dynamic_slice_in_dim(grad_modulation, (seq ^ mask) * mod_columns, mod_columns, 1), "seq", mask
        )
    own = gather_steps(own, [("dp", chip_masks()), ("dp", [1])]).reshape(dp_size * utterances, mod_columns)
    sum_mod = jnp.dot(activity.astype(F32).T, own, precision=lax.Precision.HIGHEST)
    return (output, grad_frames, grad_skip, sum_skip, sum_qkv, sum_out, sum_up, sum_down, sum_mod)


def solution(mesh):
    tokens, rows, both, turned = P("dp", "seq", None), P("dp", None), P("dp", "seq"), P("seq", "dp")
    in_specs = (tokens, tokens, tokens, both, rows, rows, both, both, turned, both, turned, both, tokens)
    out_specs = (tokens, tokens, tokens, both, both, turned, both, turned, both)
    return jax.shard_map(body, mesh=mesh, in_specs=in_specs, out_specs=out_specs, check_vma=False)
```

```python
import functools
import math

import jax
import jax.numpy as jnp
from jax import lax
from jax.experimental import pallas as pl
from jax.experimental.pallas import tpu as pltpu
from jax.sharding import Mesh
from jax.sharding import PartitionSpec as P

HEADS = 16
AXES = {"dp": ("chip", "core"), "seq": ("slow", "fast"), "all": ("chip", "core", "slow", "fast")}
CORES = 2
EPSILON = 1e-06
MASKED = -1e30
VMEM_LIMIT = 60 * 1024 * 1024
F32 = jnp.float32
BF16 = jnp.bfloat16
NT = (((1,), (1,)), ((), ()))
TN = (((0,), (0,)), ((), ()))


def dot(left, right):
    return jnp.dot(left, right, preferred_element_type=F32)


def against(left, right):
    return lax.dot_general(left, right, NT, preferred_element_type=F32)


def over_rows(left, right):
    return lax.dot_general(left, right, TN, preferred_element_type=F32)


def axis_size(axis):
    return math.prod(lax.axis_size(name) for name in AXES[axis])


def swap(values, axis, mask):
    return lax.ppermute(values, AXES[axis], [(i, i ^ mask) for i in range(axis_size(axis))])


def chip_masks():
    return [CORES * k for k in range(1, axis_size("dp") // CORES)]


def bits(axis):
    found, mask = [], CORES if axis == "dp" else 1
    while mask < axis_size(axis):
        found.append(mask)
        mask *= 2
    return found


def seq_halves():
    fast, slow = lax.axis_size("fast"), lax.axis_size("slow")
    return [list(range(1, fast)), [fast * k for k in range(1, slow)]]


def gather_steps(shard, steps):
    held = shard
    for axis, masks in steps:
        held = jnp.stack([held] + [swap(held, axis, mask) for mask in masks])
    return held


SMEM_SPEC = pl.BlockSpec(memory_space=pltpu.SMEM)
ANY_SPEC = pl.BlockSpec(memory_space=pl.ANY)


def pass_kernel(*refs):
    del refs


def after(value, *earlier):
    return pl.pallas_call(
        pass_kernel,
        out_shape=jax.ShapeDtypeStruct(value.shape, value.dtype),
        in_specs=[ANY_SPEC] * (1 + len(earlier)),
        out_specs=ANY_SPEC,
        input_output_aliases={0: 0},
        name="after",
    )(value, *earlier)


class Pieces:
    def __init__(self, arrays, masks, rows, columns):
        self.arrays, self.masks, self.rows, self.columns = arrays, masks, rows, columns


def start_gather(shard):
    return Pieces([shard[None]], [[(0, 0)]], *shard.shape)


def gather_over(held, axis, masks):
    arrays, tables = list(held.arrays), list(held.masks)
    for mask in masks:
        for array, table in zip(held.arrays, held.masks):
            arrays.append(swap(array, axis, mask))
            tables.append([(d ^ mask, s) if axis == "dp" else (d, s ^ mask) for d, s in table])
    return Pieces(arrays, tables, held.rows, held.columns)


def pack(held):
    if len(held.arrays) == 1:
        return held
    return Pieces(
        [jnp.concatenate(held.arrays)], [[entry for table in held.masks for entry in table]], held.rows, held.columns
    )


def hold(held, *earlier):
    return Pieces([after(array, *earlier) for array in held.arrays], held.masks, held.rows, held.columns)


def gather_seq(held, masks):
    held = gather_over(held, "seq", masks)
    return pack(held) if axis_size("seq") > 4 else held


def whole_columns(shard, place, relative):
    held = lax.all_gather(lax.all_gather(shard, AXES["dp"], axis=0, tiled=True), AXES["seq"], axis=0)
    if relative:
        held = jnp.take(held, jnp.arange(held.shape[0]) ^ place[1], axis=0)
    full = jnp.moveaxis(held, 0, 1).reshape(held.shape[1], -1)
    return Pieces([full], None, *full.shape)


def narrow(shard):
    return shard.shape[1] % 128 != 0


class Bank:
    def __init__(self, array, start, columns):
        self.arrays, self.start, self.columns = [array], start, columns
        self.rows = array.shape[1]


def bank_copies(bank, ref, seq, first, columns, target, sems, column):
    seqs, found = axis_size("seq"), []
    for owner in range(bank.arrays[0].shape[0] // seqs):
        source = ref.at[owner * seqs + seq, :, pl.ds(bank.start + first, columns)]
        spot = target.at[pl.ds(owner * bank.rows, bank.rows), pl.ds(column, columns)]
        found.append(pltpu.make_async_copy(source, spot, sems.at[len(found)]))
    return found


def pack_kernel(*refs):
    *head, w_up_ref, w_down_ref, _, _, bank_ref = refs
    parts = [ref[...].T for ref in head] + [w_up_ref[...], w_down_ref[...].T]
    bank_ref[...] = jnp.concatenate(parts, 1)


def pack_bank(earlier, too, *weights):
    rows = weights[-2].shape[0]
    return pl.pallas_call(
        pack_kernel,
        out_shape=jax.ShapeDtypeStruct((rows, sum(weight.size for weight in weights) // rows), BF16),
        in_specs=[pl.BlockSpec(memory_space=pltpu.VMEM)] * len(weights) + [ANY_SPEC] * 2,
        compiler_params=pltpu.CompilerParams(vmem_limit_bytes=VMEM_LIMIT),
        name="pack_bank",
    )(*weights, earlier, too)


def unpack_kernel(chunk, sums_ref, up_ref, down_ref):
    for part in range(up_ref.shape[1] // chunk):
        start = 2 * part * chunk
        span = slice(part * chunk, (part + 1) * chunk)
        up_ref[:, span] = sums_ref[:, start : start + chunk].astype(F32)
        down_ref[span, :] = sums_ref[:, start + chunk : start + 2 * chunk].astype(F32).T


def unpack_sums(sums, units, chunk):
    rows = sums.shape[0]
    return pl.pallas_call(
        functools.partial(unpack_kernel, chunk),
        out_shape=tuple(jax.ShapeDtypeStruct(shape, F32) for shape in [(rows, units), (units, rows)]),
        compiler_params=pltpu.CompilerParams(vmem_limit_bytes=VMEM_LIMIT),
        name="unpack_sums",
    )(sums)


def weight_copies(pieces, refs, target, sems, place_ref, relative):
    if isinstance(pieces, Bank):
        copies, seqs = [], axis_size("seq")
        per_seq = pieces.arrays[0].shape[0] // seqs
        for seq in range(seqs):
            column = pl.multiple_of((place_ref[1] ^ seq) * pieces.columns, pieces.columns)
            part_sems = sems.at[pl.ds(seq * per_seq, per_seq)]
            copies += bank_copies(pieces, refs[0], seq, 0, pieces.columns, target, part_sems, column)
        return copies
    if pieces.masks is None:
        return [pltpu.make_async_copy(refs[0], target, sems.at[0])]
    copies, rows, columns = [], pieces.rows, pieces.columns
    for ref, table in zip(refs, pieces.masks):
        for entry, (dp_mask, seq_mask) in enumerate(table):
            row = pl.multiple_of((place_ref[0] ^ dp_mask) * rows, rows)
            target_rows = target.at[pl.ds(row, rows), :]
            if target.shape[1] != columns:
                if relative:
                    column = seq_mask * columns
                else:
                    column = pl.multiple_of((place_ref[1] ^ seq_mask) * columns, columns)
                target_rows = target.at[pl.ds(row, rows), pl.ds(column, columns)]
            copies.append(pltpu.make_async_copy(ref.at[entry], target_rows, sems.at[len(copies)]))
    return copies


def copy_count(pieces):
    if isinstance(pieces, Bank):
        return pieces.arrays[0].shape[0]
    return 1 if pieces.masks is None else sum(len(table) for table in pieces.masks)


def assemble_kernel(pieces, place_ref, *rest):
    refs, out_ref, sems = rest[:-2], rest[-2], rest[-1]
    copies = weight_copies(pieces, refs, out_ref, sems, place_ref, False)
    for copy in copies:
        copy.start()
    for copy in copies:
        copy.wait()


def assemble(pieces, place, shape):
    return pl.pallas_call(
        functools.partial(assemble_kernel, pieces),
        out_shape=jax.ShapeDtypeStruct(shape, BF16),
        in_specs=[SMEM_SPEC] + [ANY_SPEC] * len(pieces.arrays),
        out_specs=pl.BlockSpec(memory_space=pltpu.VMEM),
        scratch_shapes=[pltpu.SemaphoreType.DMA((copy_count(pieces),))],
        compiler_params=pltpu.CompilerParams(vmem_limit_bytes=VMEM_LIMIT),
        cost_estimate=pl.CostEstimate(flops=0, bytes_accessed=4 * math.prod(shape), transcendentals=0),
        name="assemble",
    )(place, *pieces.arrays)


def send_seq(held):
    total = held[0]
    for mask in range(1, held.shape[0]):
        total = total + swap(held[mask].astype(BF16), "seq", mask).astype(F32)
    return total


def send_chips(held):
    total = held[0]
    for mask in chip_masks():
        total = total + swap(held[mask // CORES].astype(BF16), "dp", mask).astype(F32)
    return total


def halve_chips(held):
    for mask in reversed(bits("dp")):
        count = held.shape[0] // 2
        held = held[:count] + swap(held[count:].astype(BF16), "dp", mask).astype(F32)
    return held[0]


def add_cores(keep, give):
    return keep.astype(F32) + swap(give, "dp", 1).astype(F32)


def split_rows(place_ref, source_ref, rows, chip, core, by_mask):
    owner = place_ref[0] ^ (chip * CORES + core) if by_mask else chip * CORES + (place_ref[0] % CORES ^ core)
    return source_ref[pl.ds(pl.multiple_of(owner * rows, rows), rows), :]


def weight_grad_kernel(count, seqs, by_mask, place_ref, *rest):
    x_refs, y_ref, (keep_ref, give_ref, xt_ref) = rest[:count], rest[count], rest[-3:]
    chip = pl.program_id(0)
    per_piece = len(y_ref.shape) == 3
    rows, columns = keep_ref.shape[-2:]
    wide = x_refs[0].shape[1]

    @pl.when(chip == 0)
    def _():
        for piece, ref in enumerate(x_refs):
            if per_piece:
                xt_ref[:, piece * ref.shape[0] : (piece + 1) * ref.shape[0]] = ref[...].T
            else:
                xt_ref[piece * wide : (piece + 1) * wide, :] = ref[...].T

    y = y_ref[...].reshape(-1, y_ref.shape[-1])
    for core, out_ref in ((0, keep_ref), (1, give_ref)):
        result = dot(split_rows(place_ref, xt_ref, rows, chip, core, by_mask), y).astype(BF16)
        for seq in range(seqs):
            out_ref[seq, 0] = result[:, seq * columns : (seq + 1) * columns]


def weight_grad(place, xs, y, rows, seqs, by_mask, *earlier):
    chips = axis_size("dp") // CORES
    tokens, wide = xs[0].shape
    columns = y.shape[-1] // seqs
    shape = (wide, len(xs) * tokens) if y.ndim == 3 else (len(xs) * wide, tokens)
    out = jax.ShapeDtypeStruct((seqs, chips, rows, columns), BF16)
    spec = pl.BlockSpec((seqs, 1, rows, columns), lambda i: (0, i, 0, 0))
    constant = lambda array: pl.BlockSpec(array.shape, lambda i: (0,) * array.ndim)
    return pl.pallas_call(
        functools.partial(weight_grad_kernel, len(xs), seqs, by_mask),
        grid=(chips,),
        out_shape=(out, out),
        in_specs=[SMEM_SPEC] + [constant(x) for x in xs] + [constant(y)] + [ANY_SPEC] * len(earlier),
        out_specs=(spec, spec),
        scratch_shapes=[pltpu.VMEM(shape, BF16)],
        compiler_params=pltpu.CompilerParams(vmem_limit_bytes=VMEM_LIMIT),
        cost_estimate=pl.CostEstimate(
            flops=2 * math.prod(shape) * columns * seqs,
            bytes_accessed=2 * (math.prod(shape) + y.size) + 2 * shape[0] * columns * seqs,
            transcendentals=0,
        ),
        name="weight_grad",
    )(place, *xs, y, *earlier)


def qkv_kernel(width, scale, x_ref, w_ref, cos_ref, sin_ref, *rest):
    out_ref = rest[-1]
    half = width // 2
    projected = dot(x_ref[0], w_ref[...])
    cosine, sine = cos_ref[0], sin_ref[0]
    for part, factor in ((0, scale), (1, 1.0)):
        low = projected[:, part * width : part * width + half]
        high = projected[:, part * width + half : (part + 1) * width]
        out_ref[0, 0, :, part * width : part * width + half] = ((low * cosine - high * sine) * factor).astype(BF16)
        out_ref[0, 0, :, part * width + half : (part + 1) * width] = ((high * cosine + low * sine) * factor).astype(BF16)
    out_ref[0, 0, :, 2 * width :] = projected[:, 2 * width :].astype(BF16)


def project_piece(piece, normed, weights, cos_table, sin_table, held, scale):
    rows, frames, model = normed.shape
    pieces = cos_table.shape[0]
    width = weights.shape[1] // 3
    in_specs = [
        pl.BlockSpec((1, frames, model), lambda r: (r, 0, 0)),
        pl.BlockSpec((model, 3 * width), lambda r: (0, 0)),
        pl.BlockSpec((1, frames, width // 2), lambda r: (piece, 0, 0)),
        pl.BlockSpec((1, frames, width // 2), lambda r: (piece, 0, 0)),
    ]
    arrays = [normed, weights, cos_table, sin_table]
    aliases = {}
    if held is not None:
        in_specs.append(pl.BlockSpec(memory_space=pl.ANY))
        arrays.append(held)
        aliases = {4: 0}
    return pl.pallas_call(
        functools.partial(qkv_kernel, width, scale),
        grid=(rows,),
        out_shape=jax.ShapeDtypeStruct((pieces, rows, frames, 3 * width), BF16),
        in_specs=in_specs,
        out_specs=pl.BlockSpec((1, 1, frames, 3 * width), lambda r: (piece, r, 0, 0)),
        input_output_aliases=aliases,
        compiler_params=pltpu.CompilerParams(vmem_limit_bytes=VMEM_LIMIT),
        cost_estimate=pl.CostEstimate(
            flops=2 * rows * frames * model * 3 * width, bytes_accessed=5 * rows * frames * model, transcendentals=0
        ),
        name="project",
    )(*arrays)


def spread_back_kernel(grad_ref, weight_ref, *out_refs):
    piece = pl.program_id(0)
    result = against(grad_ref[0, 0], weight_ref[...]).astype(BF16)
    for position, ref in enumerate(out_refs):

        @pl.when(piece == position)
        def _():
            ref[0] = result


def spread_back(grad_qkv, weights):
    pieces, rows, frames, triple = grad_qkv.shape
    model = weights.shape[0]

    def out_spec(position):
        return pl.BlockSpec(
            (1, frames, model),
            lambda m, r: (jnp.where(m < position, 0, jnp.where(m == position, r, rows - 1)), 0, 0),
        )

    return pl.pallas_call(
        spread_back_kernel,
        grid=(pieces - 1, rows),
        out_shape=(jax.ShapeDtypeStruct((rows, frames, model), BF16),) * (pieces - 1),
        in_specs=[
            pl.BlockSpec((1, 1, frames, triple), lambda m, r: (m + 1, r, 0, 0)),
            pl.BlockSpec(weights.shape, lambda m, r: (0, 0)),
        ],
        out_specs=tuple(out_spec(position) for position in range(pieces - 1)),
        compiler_params=pltpu.CompilerParams(vmem_limit_bytes=VMEM_LIMIT),
        cost_estimate=pl.CostEstimate(
            flops=2 * (pieces - 1) * rows * frames * triple * model,
            bytes_accessed=2 * pieces * rows * frames * (triple + model),
            transcendentals=0,
        ),
        name="spread_back",
    )(grad_qkv, weights)


def head_lanes(shape, heads, width, split):
    lane = lax.broadcasted_iota(jnp.int32, shape, 1)
    size = width // heads
    if split:
        return (lane % (width // 2)) // (size // 2)
    return lane // size


def spread_back_kernel(grad_ref, weight_ref, *out_refs):
    piece = pl.program_id(0)
    result = against(grad_ref[0, 0], weight_ref[...]).astype(BF16)
    for position, ref in enumerate(out_refs):

        @pl.when(piece == position)
        def _():
            ref[0] = result


def spread_back(grad_qkv, weights):
    pieces, rows, frames, triple = grad_qkv.shape
    model = weights.shape[0]

    def out_spec(position):
        return pl.BlockSpec(
            (1, frames, model),
            lambda m, r: (jnp.where(m < position, 0, jnp.where(m == position, r, rows - 1)), 0, 0),
        )

    return pl.pallas_call(
        spread_back_kernel,
        grid=(pieces - 1, rows),
        out_shape=(jax.ShapeDtypeStruct((rows, frames, model), BF16),) * (pieces - 1),
        in_specs=[
            pl.BlockSpec((1, 1, frames, triple), lambda m, r: (m + 1, r, 0, 0)),
            pl.BlockSpec(weights.shape, lambda m, r: (0, 0)),
        ],
        out_specs=tuple(out_spec(position) for position in range(pieces - 1)),
        compiler_params=pltpu.CompilerParams(vmem_limit_bytes=VMEM_LIMIT),
        cost_estimate=pl.CostEstimate(
            flops=2 * (pieces - 1) * rows * frames * triple * model,
            bytes_accessed=2 * pieces * rows * frames * (triple + model),
            transcendentals=0,
        ),
        name="spread_back",
    )(grad_qkv, weights)


def head_lanes(shape, heads, width, split):
    lane = lax.broadcasted_iota(jnp.int32, shape, 1)
    size = width // heads
    if split:
        return (lane % (width // 2)) // (size // 2)
    return lane // size


def column_of(row, lanes):
    return jnp.broadcast_to(row, (128, row.shape[1])).T[:, :lanes]


def attend_kernel(heads, width, qkv_ref, seg_ref, *rest):
    pieces, _, frames, _ = qkv_ref.shape
    out_refs, (lse_ref, vt_ref, ot_ref, seg_col_ref) = rest[:pieces], rest[pieces:]
    length = pieces * frames
    step = pl.program_id(1)
    size = width // heads
    keys = qkv_ref[:, 0, :, width : 2 * width].reshape(length, width)

    @pl.when(step == 0)
    def _():
        vt_ref[...] = qkv_ref[:, 0, :, 2 * width :].reshape(length, width).T
        for piece in range(pieces):
            seg_col_ref[piece * frames : (piece + 1) * frames, :] = column_of(seg_ref[0, piece : piece + 1, :], 128)

    queries = qkv_ref[step, 0, :, :width]
    owner = head_lanes((frames, width), heads, width, True)
    allowed = seg_col_ref[:, :1] == seg_ref[0, pl.ds(step, 1), :]
    for head in range(heads):
        masked = jnp.where(owner == head, queries, jnp.zeros_like(queries))
        scores = jnp.where(allowed, against(keys, masked), MASKED)
        highest = jnp.max(scores, 0, keepdims=True)
        raised = jnp.exp(scores - highest)
        total = jnp.sum(raised, 0, keepdims=True)
        lse_ref[0, 0, head : head + 1, :] = highest + jnp.log(total)
        result = dot(vt_ref[head * size : (head + 1) * size, :], raised.astype(BF16))
        ot_ref[head * size : (head + 1) * size, :] = result / total
    result = ot_ref[...].T.astype(BF16)
    for piece in range(pieces):

        @pl.when(step == piece)
        def _():
            out_refs[piece][0] = result


def attend(qkv, seg, heads):
    pieces, rows, frames, triple = qkv.shape
    width = triple // 3
    length = pieces * frames
    results = pl.pallas_call(
        functools.partial(attend_kernel, heads, width),
        grid=(rows, pieces),
        out_shape=(jax.ShapeDtypeStruct((rows, frames, width), BF16),) * pieces
        + (jax.ShapeDtypeStruct((rows, pieces, heads, frames), F32),),
        in_specs=[
            pl.BlockSpec((pieces, 1, frames, triple), lambda r, s: (0, r, 0, 0)),
            pl.BlockSpec((1, pieces, frames), lambda r, s: (r, 0, 0)),
        ],
        out_specs=(pl.BlockSpec((1, frames, width), lambda r, s: (r, 0, 0)),) * pieces
        + (pl.BlockSpec((1, 1, heads, frames), lambda r, s: (r, s, 0, 0)),),
        scratch_shapes=[
            pltpu.VMEM((width, length), BF16),
            pltpu.VMEM((width, frames), F32),
            pltpu.VMEM((length, 128), F32),
        ],
        compiler_params=pltpu.CompilerParams(vmem_limit_bytes=VMEM_LIMIT),
        cost_estimate=pl.CostEstimate(
            flops=4 * rows * length * length * 256 * heads,
            bytes_accessed=8 * rows * length * width,
            transcendentals=rows * heads * length * length,
        ),
        name="attend",
    )(qkv, seg)
    return results[:pieces], results[pieces]


def attend_back_kernel(heads, width, scale, qkv_ref, seg_ref, lse_ref, cos_ref, sin_ref, *rest):
    pieces, _, frames, _ = qkv_ref.shape
    out_refs, grad_refs = rest[:pieces], rest[pieces : 2 * pieces]
    result_ref, kt_ref, dk_ref, dv_ref, dqt_ref, seg_col_ref, out_ref, grad_ref = rest[2 * pieces :]
    length = pieces * frames
    step = pl.program_id(1)
    size, half = width // heads, width // 2
    keys = qkv_ref[:, 0, :, width : 2 * width].reshape(length, width)
    values = qkv_ref[:, 0, :, 2 * width :].reshape(length, width)

    @pl.when(step == 0)
    def _():
        kt_ref[...] = keys.T
        dk_ref[...] = jnp.zeros_like(dk_ref)
        dv_ref[...] = jnp.zeros_like(dv_ref)
        for piece in range(pieces):
            seg_col_ref[piece * frames : (piece + 1) * frames, :] = column_of(seg_ref[0, piece : piece + 1, :], 128)
            out_ref[piece] = out_refs[piece][0]
            grad_ref[piece] = grad_refs[piece][0]

    queries = qkv_ref[step, 0, :, :width]
    grad = grad_ref[step]
    query_owner = head_lanes((frames, width), heads, width, True)
    value_owner = head_lanes((frames, width), heads, width, False)
    allowed = seg_col_ref[:, :1] == seg_ref[0, pl.ds(step, 1), :]
    product = grad.astype(F32) * out_ref[step].astype(F32)
    picker = lax.broadcasted_iota(jnp.int32, (8, width), 1) // size == lax.broadcasted_iota(jnp.int32, (8, width), 0)
    inner = lax.dot_general(
        picker.astype(F32), product, NT, precision=lax.Precision.HIGHEST, preferred_element_type=F32
    )
    for head in range(heads):
        masked = jnp.where(query_owner == head, queries, jnp.zeros_like(queries))
        masked_grad = jnp.where(value_owner == head, grad, jnp.zeros_like(grad))
        scores = against(keys, masked)
        weights = jnp.where(allowed, jnp.exp(scores - lse_ref[0, 0, head : head + 1, :]), 0.0)
        grad_weights = against(values, masked_grad)
        grad_scores = (weights * (grad_weights - inner[head : head + 1, :])).astype(BF16)
        dv_ref[...] += dot(weights.astype(BF16), masked_grad)
        dk_ref[...] += dot(grad_scores, masked)
        low, high = head * size // 2, half + head * size // 2
        head_keys = jnp.concatenate([kt_ref[low : low + size // 2, :], kt_ref[high : high + size // 2, :]], 0)
        part = dot(head_keys, grad_scores)
        dqt_ref[low : low + size // 2, :] = part[: size // 2]
        dqt_ref[high : high + size // 2, :] = part[size // 2 :]

    def unrotate(values, cosine, sine):
        low, high = values[:, :half], values[:, half:]
        return (low * cosine + high * sine).astype(BF16), (high * cosine - low * sine).astype(BF16)

    low, high = unrotate(dqt_ref[...].T * scale, cos_ref[step], sin_ref[step])
    result_ref[step, 0, :, :half] = low
    result_ref[step, 0, :, half:width] = high

    @pl.when(step == pieces - 1)
    def _():
        for piece in range(pieces):
            span = slice(piece * frames, (piece + 1) * frames)
            low, high = unrotate(dk_ref[span, :], cos_ref[piece], sin_ref[piece])
            result_ref[piece, 0, :, width : width + half] = low
            result_ref[piece, 0, :, width + half : 2 * width] = high
            result_ref[piece, 0, :, 2 * width :] = dv_ref[span, :].astype(BF16)


def attend_back(qkv, seg, lse, cos_table, sin_table, outs, grads, heads, scale):
    pieces, rows, frames, triple = qkv.shape
    width = triple // 3
    length = pieces * frames
    whole = pl.BlockSpec((pieces, 1, frames, triple), lambda r, s: (0, r, 0, 0))
    table = pl.BlockSpec((pieces, frames, width // 2), lambda r, s: (0, 0, 0))
    block = pl.BlockSpec((1, frames, width), lambda r, s: (r, 0, 0))
    return pl.pallas_call(
        functools.partial(attend_back_kernel, heads, width, scale),
        grid=(rows, pieces),
        out_shape=jax.ShapeDtypeStruct(qkv.shape, BF16),
        in_specs=[
            whole,
            pl.BlockSpec((1, pieces, frames), lambda r, s: (r, 0, 0)),
            pl.BlockSpec((1, 1, heads, frames), lambda r, s: (r, s, 0, 0)),
            table,
            table,
        ]
        + [block] * (2 * pieces),
        out_specs=whole,
        scratch_shapes=[
            pltpu.VMEM((width, length), BF16),
            pltpu.VMEM((length, width), F32),
            pltpu.VMEM((length, width), F32),
            pltpu.VMEM((width, frames), F32),
            pltpu.VMEM((length, 128), F32),
            pltpu.VMEM((pieces, frames, width), BF16),
            pltpu.VMEM((pieces, frames, width), BF16),
        ],
        compiler_params=pltpu.CompilerParams(vmem_limit_bytes=VMEM_LIMIT),
        cost_estimate=pl.CostEstimate(
            flops=10 * rows * length * length * 256 * heads,
            bytes_accessed=16 * rows * length * width,
            transcendentals=rows * heads * length * length,
        ),
        name="attend_back",
    )(qkv, seg, lse, cos_table, sin_table, *outs, *grads)


def mlp_kernel(bank, chunk, place_ref, normed_ref, grad_ref, bank_ref, *rest):
    fed_ref, gn_ref, grads_ref, nt_ref, gt_ref, weight_ref, result_ref, sems = rest
    step, rows = pl.program_id(0), bank.rows
    units = bank.columns // 2
    per_place = units // chunk
    half = bank.arrays[0].shape[0] // axis_size("seq")

    def copies(block, slot):
        start = (block % per_place) * chunk
        target, found = weight_ref.at[slot], []
        for which in range(2):
            found += bank_copies(
                bank, bank_ref, block // per_place, which * units + start, chunk, target,
                sems.at[slot, pl.ds(which * half, half)], which * chunk,
            )
        return found

    @pl.when(step == 0)
    def _():
        for copy in copies(0, 0):
            copy.start()
        nt_ref[...] = normed_ref[...].T
        gt_ref[...] = grad_ref[...].T
        fed_ref[...] = jnp.zeros_like(fed_ref)
        gn_ref[...] = jnp.zeros_like(gn_ref)

    for block in range(1, axis_size("seq") * per_place):

        @pl.when(step + 1 == block)
        def _():
            for copy in copies(block, block % 2):
                copy.start()

    slot = step % 2
    for copy in copies(0, slot):
        copy.wait()
    up, down = weight_ref[slot, :, :chunk], weight_ref[slot, :, chunk:]
    before = dot(normed_ref[...], up)
    square = before * before
    factor = math.sqrt(2.0 / math.pi)
    bent = jnp.tanh(factor * (before + 0.044715 * (square * before)))
    activated = (0.5 * before * (1.0 + bent)).astype(BF16)
    slope = 0.5 * (1.0 + bent) + 0.5 * before * (1.0 - bent * bent) * (factor * (1.0 + 3 * 0.044715 * square))
    grad_before = (dot(grad_ref[...], down) * slope).astype(BF16)
    fed_ref[...] += against(activated, down)
    gn_ref[...] += against(grad_before, up)
    result_ref[:, :chunk] = dot(nt_ref[...], grad_before).astype(BF16)
    result_ref[:, chunk:] = dot(gt_ref[...], activated).astype(BF16)
    for chip in range(grads_ref.shape[2]):
        for core in range(CORES):
            owner = chip * CORES + core
            grads_ref[core, 0, chip] = result_ref[owner * rows : (owner + 1) * rows, :]


def mlp(place, normed, grad, bank):
    tokens, model = normed.shape
    seqs, chips = axis_size("seq"), axis_size("dp") // CORES
    units = bank.columns // 2
    chunk = min(512, units)
    per_place = units // chunk
    whole = pl.BlockSpec((tokens, model), lambda i: (0, 0))
    hidden = seqs * units
    return pl.pallas_call(
        functools.partial(mlp_kernel, bank, chunk),
        grid=(seqs * per_place,),
        out_shape=(jax.ShapeDtypeStruct((tokens, model), F32),) * 2
        + (jax.ShapeDtypeStruct((CORES, seqs, chips, bank.rows, 2 * units), BF16),),
        in_specs=[SMEM_SPEC, whole, whole, ANY_SPEC],
        out_specs=(
            whole,
            whole,
            pl.BlockSpec(
                (CORES, 1, chips, bank.rows, 2 * chunk), lambda i: (0, i // per_place, 0, 0, i % per_place)
            ),
        ),
        scratch_shapes=[
            pltpu.VMEM((model, tokens), BF16),
            pltpu.VMEM((model, tokens), BF16),
            pltpu.VMEM((2, model, 2 * chunk), BF16),
            pltpu.VMEM((model, 2 * chunk), BF16),
            pltpu.SemaphoreType.DMA((2, 2 * CORES * chips)),
        ],
        compiler_params=pltpu.CompilerParams(vmem_limit_bytes=VMEM_LIMIT),
        cost_estimate=pl.CostEstimate(
            flops=12 * tokens * model * hidden,
            bytes_accessed=8 * model * hidden + 12 * tokens * model,
            transcendentals=tokens * hidden,
        ),
        name="mlp",
    )(place, normed, grad, *bank.arrays)


def standardize(values):
    centre = values - jnp.mean(values, -1, keepdims=True)
    inverse = lax.rsqrt(jnp.mean(centre * centre, -1, keepdims=True) + EPSILON)
    return centre * inverse, inverse


def standardize_back(grad, standard, inverse):
    return inverse * (
        grad - jnp.mean(grad, -1, keepdims=True) - standard * jnp.mean(grad * standard, -1, keepdims=True)
    )


def utterance_of(seg_ref):
    return column_of(seg_ref[0], 1)


def by_frame(owner, mod_ref, part):
    count = mod_ref.shape[1]
    result = mod_ref[0, count - 1, part : part + 1, :]
    for position in range(count - 2, -1, -1):
        result = jnp.where(owner == float(position), mod_ref[0, position, part : part + 1, :], result)
    return result


def add_up(owner, values, out_ref, part, count):
    for position in range(count):
        out_ref[0, part, position : position + 1, :] = jnp.sum(
            jnp.where(owner == float(position), values, 0.0), 0, keepdims=True
        )


def load_weight(pieces, refs, target, sems, place_ref, relative):
    @pl.when(pl.program_id(0) == 0)
    def _():
        copies = weight_copies(pieces, refs, target, sems, place_ref, relative)
        for copy in copies:
            copy.start()
        for copy in copies:
            copy.wait()


def row_call(kernel, name, place, rows, by_row, fixed, pieces, weight_shape, outs, flops, earlier=()):
    row_spec = lambda shape: pl.BlockSpec((1,) + tuple(shape[1:]), lambda r: (r,) + (0,) * (len(shape) - 1))
    fixed_specs = [pl.BlockSpec(array.shape, lambda r, n=array.ndim: (0,) * n) for array in fixed]
    scalars = [array for array in place]
    size = sum(array.size * array.dtype.itemsize for array in by_row) + 2 * math.prod(weight_shape)
    return pl.pallas_call(
        kernel,
        grid=(rows,),
        out_shape=tuple(outs),
        in_specs=[SMEM_SPEC] * len(scalars)
        + [row_spec(array.shape) for array in by_row]
        + fixed_specs
        + [ANY_SPEC] * (len(pieces.arrays) + len(earlier)),
        out_specs=tuple(row_spec(out.shape) for out in outs),
        scratch_shapes=[pltpu.VMEM(weight_shape, BF16), pltpu.SemaphoreType.DMA((copy_count(pieces),))],
        compiler_params=pltpu.CompilerParams(vmem_limit_bytes=VMEM_LIMIT),
        cost_estimate=pl.CostEstimate(flops=flops, bytes_accessed=2 * size, transcendentals=0),
        name=name,
    )(*scalars, *by_row, *fixed, *pieces.arrays, *earlier)


def enter_kernel(pieces, place_ref, coef_ref, frames_ref, skip_ref, cond_ref, seg_ref, mod_ref, *rest):
    refs, (hidden_ref, normed_ref, weight_ref, sems) = rest[:-4], rest[-4:]
    load_weight(pieces, refs, weight_ref, sems, place_ref, False)
    row, model = pl.program_id(0), frames_ref.shape[2]
    owner = utterance_of(seg_ref)
    count = mod_ref.shape[1]
    factor = coef_ref[row, count - 1]
    for position in range(count - 2, -1, -1):
        factor = jnp.where(owner == float(position), coef_ref[row, position], factor)
    hidden = dot(frames_ref[0], weight_ref[:model, :]) + dot(skip_ref[0], weight_ref[model:, :])
    hidden = hidden + factor * cond_ref[0].astype(F32)
    hidden_ref[0] = hidden
    standard, _ = standardize(hidden)
    normed_ref[0] = (standard * (1.0 + by_frame(owner, mod_ref, 1)) + by_frame(owner, mod_ref, 0)).astype(BF16)


def branch_kernel(pieces, count, place_ref, *rest):
    blocks, (hidden_ref, cot_ref, seg_ref, mod_ref) = rest[:count], rest[count : count + 4]
    refs = rest[count + 4 : -7]
    attn_ref, branch_ref, middle_ref, normed_ref, grad_ref, weight_ref, sems = rest[-7:]
    load_weight(pieces, refs, weight_ref, sems, place_ref, True)
    owner = utterance_of(seg_ref)
    attn = jnp.concatenate([block[0] for block in blocks], -1)
    attn_ref[0] = attn
    branch = against(attn, weight_ref[...])
    branch_ref[0] = branch
    middle = hidden_ref[0] + by_frame(owner, mod_ref, 2) * branch
    middle_ref[0] = middle
    standard, _ = standardize(middle)
    normed_ref[0] = (standard * (1.0 + by_frame(owner, mod_ref, 4)) + by_frame(owner, mod_ref, 3)).astype(BF16)
    grad_ref[0] = (by_frame(owner, mod_ref, 5) * cot_ref[0].astype(F32)).astype(BF16)


def middle_back_kernel(pieces, seqs, place_ref, middle_ref, fed_ref, gn_ref, cot_ref, branch_ref, seg_ref, mod_ref, *rest):
    refs = rest[: len(pieces.arrays)]
    output_ref, grad_ref, grad_branch_ref, sums_ref = rest[len(refs) : len(refs) + 4]
    block_refs, (weight_ref, sems) = rest[len(refs) + 4 : -2], rest[-2:]
    load_weight(pieces, refs, weight_ref, sems, place_ref, True)
    owner, count = utterance_of(seg_ref), mod_ref.shape[1]
    middle, fed, grad_norm, grad_out = middle_ref[0], fed_ref[0], gn_ref[0], cot_ref[0].astype(F32)
    output_ref[0] = (middle + by_frame(owner, mod_ref, 5) * fed).astype(BF16)
    standard, inverse = standardize(middle)
    grad_middle = grad_out + standardize_back(grad_norm * (1.0 + by_frame(owner, mod_ref, 4)), standard, inverse)
    grad_ref[0] = grad_middle
    grad_branch = (by_frame(owner, mod_ref, 2) * grad_middle).astype(BF16)
    grad_branch_ref[0] = grad_branch
    grad_attn = dot(grad_branch, weight_ref[...]).astype(BF16)
    width = grad_attn.shape[1] // seqs
    for seq in range(seqs):
        block_refs[seq][0] = grad_attn[:, seq * width : (seq + 1) * width]
    add_up(owner, grad_middle * branch_ref[0], sums_ref, 0, count)
    add_up(owner, grad_norm, sums_ref, 1, count)
    add_up(owner, grad_norm * standard, sums_ref, 2, count)
    add_up(owner, grad_out * fed, sums_ref, 3, count)


def leave_kernel(pieces, seqs, place_ref, hidden_ref, grad_middle_ref, own_ref, *rest):
    got = rest[: seqs - 1]
    seg_ref, mod_ref, qkv_ref = rest[seqs - 1 : seqs + 2]
    refs = rest[seqs + 2 : seqs + 2 + len(pieces.arrays)]
    columns_ref, frames_ref, skip_ref, sums_ref, weight_ref, sems = rest[-6:]
    load_weight(pieces, refs, weight_ref, sems, place_ref, False)
    owner, count = utterance_of(seg_ref), mod_ref.shape[1]
    grad_norm = against(own_ref[0], qkv_ref[...])
    for ref in got:
        grad_norm = grad_norm + ref[0].astype(F32)
    standard, inverse = standardize(hidden_ref[0])
    grad = standardize_back(grad_norm * (1.0 + by_frame(owner, mod_ref, 1)), standard, inverse)
    grad_hidden = (grad_middle_ref[0] + grad).astype(BF16)
    model = grad_hidden.shape[1]
    frames_ref[0] = against(grad_hidden, weight_ref[:model, :]).astype(BF16)
    skip_ref[0] = against(grad_hidden, weight_ref[model:, :]).astype(BF16)
    add_up(owner, grad_norm, sums_ref, 0, count)
    add_up(owner, grad_norm * standard, sums_ref, 1, count)
    width = model // seqs
    turned = grad_hidden.astype(F32)
    bit = 1
    while bit < seqs:
        parts = [turned[:, (s ^ bit) * width : ((s ^ bit) + 1) * width] for s in range(seqs)]
        turned = jnp.where((place_ref[1] // bit) % 2 == 1, jnp.concatenate(parts, -1), turned)
        bit *= 2
    columns_ref[0] = turned.astype(BF16)


def time_embed(flow_values, model_width):
    half_dim = model_width // 2
    frequency = jnp.exp(jnp.arange(half_dim, dtype=F32) * (-math.log(10000.0) / half_dim))
    angles = 1000.0 * flow_values[..., None] * frequency
    return jnp.concatenate([jnp.sin(angles), jnp.cos(angles)], -1)


def body(
    frames, skip_in, cond, seg_ids, drop_flags, flow_times, w_skip, w_qkv, w_out, w_up, w_down, w_mod, cotangent
):
    row_count, frame_count, model = frames.shape
    seq_size, dp_size = axis_size("seq"), axis_size("dp")
    chips = dp_size // CORES
    dp, seq = lax.axis_index(AXES["dp"]), lax.axis_index(AXES["seq"])
    place = jnp.stack([dp, seq]).astype(jnp.int32)
    head_dim = model // HEADS
    heads = HEADS // seq_size
    width = heads * head_dim
    half = head_dim // 2
    scale = head_dim ** (-0.5)
    tokens = row_count * frame_count
    segs = drop_flags.shape[1]
    frame_shape = (row_count, frame_count, model)
    partners = range(1, seq_size)
    fast, slow = seq_halves()
    rows = w_up.shape[0]
    shape_of = jax.ShapeDtypeStruct

    by_head = w_qkv.reshape(w_qkv.shape[0], heads, 3, 2, half)
    qkv_shard = jnp.concatenate(
        [
            by_head[:, :, 0].swapaxes(1, 2).reshape(-1, width),
            by_head[:, :, 1].swapaxes(1, 2).reshape(-1, width),
            by_head[:, :, 2].reshape(-1, width),
        ],
        1,
    )
    skip_parts = pack(gather_over(start_gather(w_skip), "dp", chip_masks()))

    skip_near = skip_parts.arrays[0]

    small = jnp.concatenate([flow_times, drop_flags.astype(F32)], 1)
    small = gather_steps(small, [("dp", [mask]) for mask in bits("dp") + [1]])
    small = small.reshape((CORES, chips) + small.shape[-2:])
    dropped = jnp.sum(small[..., segs:])
    slots = float(row_count * segs * dp_size)
    cond_scale = slots / jnp.maximum(slots - dropped, 1.0)
    utterances = row_count * segs
    activity = jax.nn.silu(time_embed(small[..., :segs], model)).astype(BF16).reshape(dp_size * utterances, model)
    mod_rows, mod_columns = w_mod.shape
    activity = lax.dynamic_slice_in_dim(activity, dp * mod_rows, mod_rows, 1)
    coefficients = (1.0 - drop_flags.astype(F32)) * cond_scale

    if narrow(w_skip):
        skip_parts = whole_columns(w_skip, place, False)
        arrived = skip_parts.arrays[0]
    else:
        skip_parts = gather_over(skip_parts, "seq", partners)
        arrived = skip_parts.arrays[-1]
        skip_parts = gather_over(skip_parts, "dp", [1])

    partial = dot(activity, w_mod).reshape(CORES, chips, utterances, mod_columns)
    modulation = partial[0] + swap(partial[1], "dp", 1)
    for mask in reversed(bits("dp")):
        count = modulation.shape[0] // 2
        modulation = modulation[:count] + swap(modulation[count:], "dp", mask)
    modulation = modulation[0]
    extra = -(-tokens // mod_columns)
    numbers = jnp.pad(seg_ids.astype(F32).reshape(-1), (0, extra * mod_columns - tokens)).reshape(extra, mod_columns)
    own_mod = jnp.concatenate([modulation, numbers])
    all_mod = jnp.stack([own_mod] + [swap(own_mod, "seq", mask) for mask in partners])
    segments = all_mod[:, utterances:].reshape(seq_size, -1)[:, :tokens].reshape(seq_size, row_count, frame_count)
    segments = segments.swapaxes(0, 1)
    modulation = jnp.take(all_mod[:, :utterances], jnp.arange(seq_size) ^ seq, axis=0)
    modulation = modulation.swapaxes(0, 1).reshape(row_count, segs, 6, model)
    seg_here = segments[:, :1]

    units = w_up.shape[1]
    if narrow(w_out.T):
        out_parts = whole_columns(w_out.T, place, True)
        bank = pack_bank(arrived, all_mod, w_up, w_down)
    else:
        bank = pack_bank(arrived, all_mod, w_out, w_up, w_down)
    bank = lax.all_gather(bank, AXES["all"], axis=0)
    lead = bank.shape[2] - 2 * units
    if lead:
        out_parts = Bank(bank, 0, lead)
    bank = Bank(bank, lead, 2 * units)

    qkv_full = assemble(
        gather_over(pack(gather_over(start_gather(after(qkv_shard, arrived)), "dp", chip_masks())), "dp", [1]),
        place,
        (dp_size * rows, 3 * width),
    )
    hidden, normed = row_call(
        functools.partial(enter_kernel, skip_parts),
        "enter",
        [place, coefficients],
        row_count,
        [frames, skip_in, cond, seg_here, modulation],
        [],
        skip_parts,
        (2 * model, model),
        [shape_of(frame_shape, F32), shape_of(frame_shape, BF16)],
        4 * tokens * model * model,
    )

    positions = (jnp.arange(seq_size) ^ seq)[:, None] * frame_count + jnp.arange(frame_count)
    frequency = jnp.exp((jnp.arange(width // 2) % half).astype(F32) * (-2.0 * math.log(10000.0) / head_dim))
    angles = positions.astype(F32)[..., None] * frequency
    cos_table, sin_table = jnp.cos(angles), jnp.sin(angles)

    pieces = [normed] + [swap(normed, "seq", mask) for mask in partners]
    qkv = None
    for position, piece in enumerate(pieces):
        qkv = project_piece(position, piece, qkv_full, cos_table, sin_table, qkv, scale)

    attended, lse = attend(qkv, segments, heads)
    blocks = [attended[0]] + [swap(attended[mask], "seq", mask) for mask in partners]
    attn, branch, middle, normed_two, grad_fed = row_call(
        functools.partial(branch_kernel, out_parts, seq_size),
        "branch",
        [place],
        row_count,
        blocks + [hidden, cotangent, seg_here, modulation],
        [],
        out_parts,
        (model, model),
        [
            shape_of(frame_shape, BF16),
            shape_of(frame_shape, F32),
            shape_of(frame_shape, F32),
            shape_of(frame_shape, BF16),
            shape_of(frame_shape, BF16),
        ],
        2 * tokens * model * model,
    )
    fed, grad_norm_two, grad_bank = mlp(
        place, normed_two.reshape(tokens, model), grad_fed.reshape(tokens, model), bank
    )
    sum_bank = lax.psum_scatter(
        grad_bank.reshape((CORES * seq_size,) + grad_bank.shape[2:]),
        ("core",) + AXES["seq"],
        scatter_dimension=0,
        tiled=True,
    )[0]
    results = row_call(
        functools.partial(middle_back_kernel, out_parts, seq_size),
        "middle_back",
        [place],
        row_count,
        [middle, fed.reshape(frame_shape), grad_norm_two.reshape(frame_shape), cotangent, branch, seg_here, modulation],
        [],
        out_parts,
        (model, model),
        [
            shape_of(frame_shape, BF16),
            shape_of(frame_shape, F32),
            shape_of(frame_shape, BF16),
            shape_of((row_count, 4, 8, model), F32),
        ]
        + [shape_of((row_count, frame_count, width), BF16)] * seq_size,
        2 * tokens * model * model,
    )
    output, grad_middle, grad_branch, sums_two = results[:4]
    grad_heads = [results[4]] + [swap(results[4 + mask], "seq", mask) for mask in partners]
    keep_out, give_out = weight_grad(
        place, [grad_branch.reshape(tokens, model)], attn.reshape(tokens, model), rows, seq_size, True
    )
    sum_out = add_cores(keep_out, give_out)

    grad_qkv = attend_back(
        qkv, segments, lse, cos_table, sin_table, attended, grad_heads, heads, scale
    )
    flat_grad = grad_qkv.reshape(seq_size, tokens, 3 * width)
    got = [
        swap(partial, "seq", mask) for mask, partial in zip(partners, spread_back(grad_qkv, qkv_full))
    ]
    keep_qkv, give_qkv = weight_grad(
        place, [piece.reshape(tokens, model) for piece in pieces], flat_grad, rows, 1, True, got[0]
    )
    sum_out = halve_chips(send_seq(sum_out)).T
    sum_qkv = halve_chips(add_cores(keep_qkv, give_qkv)[0])
    sum_qkv = jnp.stack(
        [
            sum_qkv[:, :width].reshape(rows, 2, heads, half).swapaxes(1, 2).reshape(rows, heads, head_dim),
            sum_qkv[:, width : 2 * width].reshape(rows, 2, heads, half).swapaxes(1, 2).reshape(rows, heads, head_dim),
            sum_qkv[:, 2 * width :].reshape(rows, heads, head_dim),
        ],
        2,
    ).reshape(rows, 3 * width)

    grad_columns, grad_frames, grad_skip, sums_one = row_call(
        functools.partial(leave_kernel, skip_parts, seq_size),
        "leave",
        [place],
        row_count,
        [hidden, grad_middle, flat_grad[0].reshape(row_count, frame_count, 3 * width)]
        + got
        + [seg_here, modulation],
        [qkv_full],
        skip_parts,
        (2 * model, model),
        [
            shape_of(frame_shape, BF16),
            shape_of(frame_shape, BF16),
            shape_of(frame_shape, BF16),
            shape_of((row_count, 2, 8, model), F32),
        ],
        6 * tokens * model * model,
        [keep_qkv],
    )
    sum_bank = lax.psum_scatter(after(sum_bank, grad_columns), "chip", scatter_dimension=0, tiled=True)[0]
    sum_up, sum_down = unpack_sums(sum_bank, units, min(512, units))
    keep_skip, give_skip = weight_grad(
        place,
        [frames.reshape(tokens, model), skip_in.reshape(tokens, model)],
        grad_columns.reshape(tokens, model),
        w_skip.shape[0],
        seq_size,
        True,
    )
    sum_skip = send_chips(send_seq(add_cores(keep_skip, give_skip)))

    grad_modulation = jnp.concatenate([sums_one, sums_two], 1)[:, :, :segs]
    grad_modulation = grad_modulation.swapaxes(1, 2).reshape(utterances, 6 * model)
    own = grad_modulation
    for mask in reversed(bits("seq")):
        count = own.shape[1] // 2
        mine = (seq // mask) % 2
        keep_mod = lax.dynamic_slice_in_dim(own, mine * count, count, 1)
        own = keep_mod + swap(lax.dynamic_slice_in_dim(own, (1 - mine) * count, count, 1), "seq", mask)
    own = gather_steps(own, [("dp", [mask]) for mask in bits("dp") + [1]]).reshape(dp_size * utterances, mod_columns)
    sum_mod = jnp.dot(activity.astype(F32).T, own, precision=lax.Precision.HIGHEST)
    return (
        output,
        grad_frames,
        grad_skip,
        sum_skip,
        sum_qkv,
        sum_out,
        sum_up,
        sum_down,
        sum_mod,
    )


def solution(mesh):
    chips, seqs = mesh.shape["dp"] // CORES, mesh.shape["seq"]
    fast = 1
    while fast * fast < seqs:
        fast *= 2
    cut = Mesh(mesh.devices.reshape(chips, CORES, seqs // fast, fast), ("chip", "core", "slow", "fast"))
    dp, seq = AXES["dp"], AXES["seq"]
    tokens, rows, both, turned = P(dp, seq, None), P(dp, None), P(dp, seq), P(seq, dp)
    in_specs = (tokens, tokens, tokens, both, rows, rows, both, both, turned, both, turned, both, tokens)
    out_specs = (tokens, tokens, tokens, both, both, turned, both, turned, both)
    return jax.shard_map(body, mesh=cut, in_specs=in_specs, out_specs=out_specs, check_vma=False)
```

```python
import functools
import math

import jax
import jax.numpy as jnp
from jax import lax
from jax.experimental import pallas as pl
from jax.experimental.pallas import tpu as pltpu
from jax.sharding import Mesh
from jax.sharding import PartitionSpec as P

HEADS = 16
AXES = {"dp": ("chip", "core"), "seq": ("slow", "fast"), "all": ("chip", "core", "slow", "fast")}
CORES = 2
EPSILON = 1e-06
MASKED = -1e30
VMEM_LIMIT = 60 * 1024 * 1024
F32 = jnp.float32
BF16 = jnp.bfloat16
NT = (((1,), (1,)), ((), ()))
TN = (((0,), (0,)), ((), ()))


def dot(left, right):
    return jnp.dot(left, right, preferred_element_type=F32)


def against(left, right):
    return lax.dot_general(left, right, NT, preferred_element_type=F32)


def over_rows(left, right):
    return lax.dot_general(left, right, TN, preferred_element_type=F32)


def axis_size(axis):
    return math.prod(lax.axis_size(name) for name in AXES[axis])


def swap(values, axis, mask):
    return lax.ppermute(values, AXES[axis], [(i, i ^ mask) for i in range(axis_size(axis))])


def chip_masks():
    return [CORES * k for k in range(1, axis_size("dp") // CORES)]


def bits(axis):
    found, mask = [], CORES if axis == "dp" else 1
    while mask < axis_size(axis):
        found.append(mask)
        mask *= 2
    return found


def seq_halves():
    fast, slow = lax.axis_size("fast"), lax.axis_size("slow")
    return [list(range(1, fast)), [fast * k for k in range(1, slow)]]


def gather_steps(shard, steps):
    held = shard
    for axis, masks in steps:
        held = jnp.stack([held] + [swap(held, axis, mask) for mask in masks])
    return held


SMEM_SPEC = pl.BlockSpec(memory_space=pltpu.SMEM)
ANY_SPEC = pl.BlockSpec(memory_space=pl.ANY)


def pass_kernel(*refs):
    del refs


def after(value, *earlier):
    return pl.pallas_call(
        pass_kernel,
        out_shape=jax.ShapeDtypeStruct(value.shape, value.dtype),
        in_specs=[ANY_SPEC] * (1 + len(earlier)),
        out_specs=ANY_SPEC,
        input_output_aliases={0: 0},
        name="after",
    )(value, *earlier)


class Pieces:
    def __init__(self, arrays, masks, rows, columns):
        self.arrays, self.masks, self.rows, self.columns = arrays, masks, rows, columns


def start_gather(shard):
    return Pieces([shard[None]], [[(0, 0)]], *shard.shape)


def gather_over(held, axis, masks):
    arrays, tables = list(held.arrays), list(held.masks)
    for mask in masks:
        for array, table in zip(held.arrays, held.masks):
            arrays.append(swap(array, axis, mask))
            tables.append([(d ^ mask, s) if axis == "dp" else (d, s ^ mask) for d, s in table])
    return Pieces(arrays, tables, held.rows, held.columns)


def pack(held):
    if len(held.arrays) == 1:
        return held
    return Pieces(
        [jnp.concatenate(held.arrays)], [[entry for table in held.masks for entry in table]], held.rows, held.columns
    )


def hold(held, *earlier):
    return Pieces([after(array, *earlier) for array in held.arrays], held.masks, held.rows, held.columns)


def gather_seq(held, masks):
    held = gather_over(held, "seq", masks)
    return pack(held) if axis_size("seq") > 4 else held


def whole_columns(shard, place, relative):
    held = lax.all_gather(lax.all_gather(shard, AXES["dp"], axis=0, tiled=True), AXES["seq"], axis=0)
    if relative:
        held = jnp.take(held, jnp.arange(held.shape[0]) ^ place[1], axis=0)
    full = jnp.moveaxis(held, 0, 1).reshape(held.shape[1], -1)
    return Pieces([full], None, *full.shape)


def narrow(shard):
    return shard.shape[1] % 128 != 0


class Bank:
    def __init__(self, array, start, columns):
        self.arrays, self.start, self.columns = [array], start, columns
        self.rows = array.shape[2]


def bank_copies(bank, ref, seq, first, columns, target, sems, column):
    found = []
    for owner in range(bank.arrays[0].shape[0]):
        source = ref.at[owner, seq, :, pl.ds(bank.start + first, columns)]
        spot = target.at[pl.ds(owner * bank.rows, bank.rows), pl.ds(column, columns)]
        found.append(pltpu.make_async_copy(source, spot, sems.at[len(found)]))
    return found


def pack_kernel(count, *refs):
    *head, w_up_ref, w_down_ref = refs[:count]
    bank_ref = refs[-1]
    parts = [ref[...].T for ref in head] + [w_up_ref[...], w_down_ref[...].T]
    bank_ref[...] = jnp.concatenate(parts, 1)


def pack_bank(earlier, *weights):
    rows = weights[-2].shape[0]
    return pl.pallas_call(
        functools.partial(pack_kernel, len(weights)),
        out_shape=jax.ShapeDtypeStruct((rows, sum(weight.size for weight in weights) // rows), BF16),
        in_specs=[pl.BlockSpec(memory_space=pltpu.VMEM)] * len(weights) + [ANY_SPEC] * len(earlier),
        compiler_params=pltpu.CompilerParams(vmem_limit_bytes=VMEM_LIMIT),
        name="pack_bank",
    )(*weights, *earlier)


def unpack_kernel(chunk, sums_ref, up_ref, down_ref):
    for part in range(up_ref.shape[1] // chunk):
        start = 2 * part * chunk
        span = slice(part * chunk, (part + 1) * chunk)
        up_ref[:, span] = sums_ref[:, start : start + chunk]
        down_ref[span, :] = sums_ref[:, start + chunk : start + 2 * chunk].T


def unpack_sums(sums, units, chunk):
    rows = sums.shape[0]
    return pl.pallas_call(
        functools.partial(unpack_kernel, chunk),
        out_shape=tuple(jax.ShapeDtypeStruct(shape, F32) for shape in [(rows, units), (units, rows)]),
        compiler_params=pltpu.CompilerParams(vmem_limit_bytes=VMEM_LIMIT),
        name="unpack_sums",
    )(sums)


def weight_copies(pieces, refs, target, sems, place_ref, relative):
    if isinstance(pieces, Bank):
        copies, owners = [], pieces.arrays[0].shape[0]
        for seq in range(axis_size("seq")):
            part_sems = sems.at[pl.ds(seq * owners, owners)]
            column = pl.multiple_of((place_ref[1] ^ seq) * pieces.columns, pieces.columns)
            copies += bank_copies(pieces, refs[0], seq, 0, pieces.columns, target, part_sems, column)
        return copies
    if pieces.masks is None:
        return [pltpu.make_async_copy(refs[0], target, sems.at[0])]
    copies, rows, columns = [], pieces.rows, pieces.columns
    for ref, table in zip(refs, pieces.masks):
        for entry, (dp_mask, seq_mask) in enumerate(table):
            row = pl.multiple_of((place_ref[0] ^ dp_mask) * rows, rows)
            target_rows = target.at[pl.ds(row, rows), :]
            if target.shape[1] != columns:
                if relative:
                    column = seq_mask * columns
                else:
                    column = pl.multiple_of((place_ref[1] ^ seq_mask) * columns, columns)
                target_rows = target.at[pl.ds(row, rows), pl.ds(column, columns)]
            copies.append(pltpu.make_async_copy(ref.at[entry], target_rows, sems.at[len(copies)]))
    return copies


def copy_count(pieces):
    if isinstance(pieces, Bank):
        return axis_size("seq") * pieces.arrays[0].shape[0]
    return 1 if pieces.masks is None else sum(len(table) for table in pieces.masks)


def assemble_kernel(pieces, place_ref, *rest):
    refs, out_ref, sems = rest[:-2], rest[-2], rest[-1]
    copies = weight_copies(pieces, refs, out_ref, sems, place_ref, False)
    for copy in copies:
        copy.start()
    for copy in copies:
        copy.wait()


def assemble(pieces, place, shape):
    return pl.pallas_call(
        functools.partial(assemble_kernel, pieces),
        out_shape=jax.ShapeDtypeStruct(shape, BF16),
        in_specs=[SMEM_SPEC] + [ANY_SPEC] * len(pieces.arrays),
        out_specs=pl.BlockSpec(memory_space=pltpu.VMEM),
        scratch_shapes=[pltpu.SemaphoreType.DMA((copy_count(pieces),))],
        compiler_params=pltpu.CompilerParams(vmem_limit_bytes=VMEM_LIMIT),
        cost_estimate=pl.CostEstimate(flops=0, bytes_accessed=4 * math.prod(shape), transcendentals=0),
        name="assemble",
    )(place, *pieces.arrays)


def pick(values, index, axis):
    return lax.dynamic_index_in_dim(values, index, axis, keepdims=False)


def send_seq(held):
    total, sent = held[0], []
    for mask in range(1, held.shape[0]):
        sent.append(held[mask].astype(BF16))
        total = total + swap(sent[-1], "seq", mask).astype(F32)
    return total, sent


def send_chips(held, dtype=BF16):
    total = held[0]
    for mask in chip_masks():
        total = total + swap(held[mask // CORES].astype(dtype), "dp", mask).astype(F32)
    return total


def halve(held, axis):
    for mask in reversed(bits(axis)):
        count = held.shape[0] // 2
        held = held[:count].astype(F32) + swap(held[count:].astype(BF16), axis, mask).astype(F32)
    return held[0]


def add_cores(keep, give):
    return keep.astype(F32) + swap(give, "dp", 1).astype(F32)


def split_rows(place_ref, source_ref, rows, chip, core, by_mask):
    owner = place_ref[0] ^ (chip * CORES + core) if by_mask else chip * CORES + (place_ref[0] % CORES ^ core)
    return source_ref[pl.ds(pl.multiple_of(owner * rows, rows), rows), :]


def weight_grad_kernel(count, y_count, by_token, seqs, by_mask, place_ref, *rest):
    x_refs, y_refs, (keep_ref, give_ref, xt_ref) = rest[:count], rest[count : count + y_count], rest[-3:]
    chip = pl.program_id(0)
    rows, columns = keep_ref.shape[-2:]
    tokens, wide = x_refs[0].shape

    @pl.when(chip == 0)
    def _():
        for piece, ref in enumerate(x_refs):
            if by_token:
                xt_ref[:, piece * tokens : (piece + 1) * tokens] = ref[...].T
            else:
                xt_ref[piece * wide : (piece + 1) * wide, :] = ref[...].T

    parts = [ref[...].reshape(-1, ref.shape[-1]) for ref in y_refs]
    y = parts[0] if y_count == 1 else jnp.concatenate(parts)
    for core, out_ref in ((0, keep_ref), (1, give_ref)):
        result = dot(split_rows(place_ref, xt_ref, rows, chip, core, by_mask), y).astype(BF16)
        for seq in range(seqs):
            out_ref[seq, 0] = result[:, seq * columns : (seq + 1) * columns]


def weight_grad(place, xs, ys, by_token, rows, seqs, by_mask, *earlier):
    chips = axis_size("dp") // CORES
    tokens, wide = xs[0].shape
    columns = ys[0].shape[-1] // seqs
    shape = (wide, len(xs) * tokens) if by_token else (len(xs) * wide, tokens)
    out = jax.ShapeDtypeStruct((seqs, chips, rows, columns), BF16)
    spec = pl.BlockSpec((seqs, 1, rows, columns), lambda i: (0, i, 0, 0))
    constant = lambda array: pl.BlockSpec(array.shape, lambda i: (0,) * array.ndim)
    return pl.pallas_call(
        functools.partial(weight_grad_kernel, len(xs), len(ys), by_token, seqs, by_mask),
        grid=(chips,),
        out_shape=(out, out),
        in_specs=[SMEM_SPEC] + [constant(array) for array in list(xs) + list(ys)] + [ANY_SPEC] * len(earlier),
        out_specs=(spec, spec),
        scratch_shapes=[pltpu.VMEM(shape, BF16)],
        compiler_params=pltpu.CompilerParams(vmem_limit_bytes=VMEM_LIMIT),
        cost_estimate=pl.CostEstimate(
            flops=2 * math.prod(shape) * columns * seqs,
            bytes_accessed=2 * math.prod(shape) + 4 * shape[0] * columns * seqs,
            transcendentals=0,
        ),
        name="weight_grad",
    )(place, *xs, *ys, *earlier)


def project_kernel(pieces, width, scale, w_ref, cos_ref, sin_ref, *rest):
    x_refs, (out_ref, x_ref) = rest[:pieces], rest[pieces:]
    half = width // 2
    for piece in range(pieces):

        @pl.when(pl.program_id(0) == piece)
        def _():
            x_ref[...] = x_refs[piece][0]

    projected = dot(x_ref[...], w_ref[...])
    cosine, sine = cos_ref[0], sin_ref[0]
    for part, factor in ((0, scale), (1, 1.0)):
        low = projected[:, part * width : part * width + half]
        high = projected[:, part * width + half : (part + 1) * width]
        out_ref[0, 0, :, part * width : part * width + half] = ((low * cosine - high * sine) * factor).astype(BF16)
        out_ref[0, 0, :, part * width + half : (part + 1) * width] = ((high * cosine + low * sine) * factor).astype(BF16)
    out_ref[0, 0, :, 2 * width :] = projected[:, 2 * width :].astype(BF16)


def project(normed, weights, cos_table, sin_table, scale):
    pieces = len(normed)
    _, frames, model = normed[0].shape
    width = weights.shape[1] // 3
    table = pl.BlockSpec((1, frames, width // 2), lambda s: (s, 0, 0))
    return pl.pallas_call(
        functools.partial(project_kernel, pieces, width, scale),
        grid=(pieces,),
        out_shape=jax.ShapeDtypeStruct((pieces, 1, frames, 3 * width), BF16),
        in_specs=[pl.BlockSpec((model, 3 * width), lambda s: (0, 0)), table, table]
        + [pl.BlockSpec((1, frames, model), lambda s: (0, 0, 0))] * pieces,
        out_specs=pl.BlockSpec((1, 1, frames, 3 * width), lambda s: (s, 0, 0, 0)),
        scratch_shapes=[pltpu.VMEM((frames, model), BF16)],
        compiler_params=pltpu.CompilerParams(vmem_limit_bytes=VMEM_LIMIT),
        cost_estimate=pl.CostEstimate(
            flops=2 * pieces * frames * model * 3 * width,
            bytes_accessed=2 * pieces * frames * (model + 3 * width),
            transcendentals=0,
        ),
        name="project",
    )(weights, cos_table, sin_table, *normed)


def spread_back_kernel(count, grad_ref, weight_ref, *rest):
    out_refs = rest[-count:]
    piece = pl.program_id(0)
    result = against(grad_ref[0, 0], weight_ref[...]).astype(BF16)
    for position, ref in enumerate(out_refs):

        @pl.when(piece == position)
        def _():
            ref[0] = result


def spread_back(grad_qkv, weights, *earlier):
    pieces, rows, frames, triple = grad_qkv.shape
    model = weights.shape[0]

    def out_spec(position):
        return pl.BlockSpec(
            (1, frames, model),
            lambda m, r: (jnp.where(m < position, 0, jnp.where(m == position, r, rows - 1)), 0, 0),
        )

    return pl.pallas_call(
        functools.partial(spread_back_kernel, pieces - 1),
        grid=(pieces - 1, rows),
        out_shape=(jax.ShapeDtypeStruct((rows, frames, model), BF16),) * (pieces - 1),
        in_specs=[
            pl.BlockSpec((1, 1, frames, triple), lambda m, r: (m + 1, r, 0, 0)),
            pl.BlockSpec(weights.shape, lambda m, r: (0, 0)),
        ]
        + [ANY_SPEC] * len(earlier),
        out_specs=tuple(out_spec(position) for position in range(pieces - 1)),
        compiler_params=pltpu.CompilerParams(vmem_limit_bytes=VMEM_LIMIT),
        cost_estimate=pl.CostEstimate(
            flops=2 * (pieces - 1) * rows * frames * triple * model,
            bytes_accessed=2 * pieces * rows * frames * (triple + model),
            transcendentals=0,
        ),
        name="spread_back",
    )(grad_qkv, weights, *earlier)


def head_lanes(shape, heads, width, split):
    lane = lax.broadcasted_iota(jnp.int32, shape, 1)
    size = width // heads
    if split:
        return (lane % (width // 2)) // (size // 2)
    return lane // size


def spread_back_kernel(count, grad_ref, weight_ref, *rest):
    out_refs = rest[-count:]
    piece = pl.program_id(0)
    result = against(grad_ref[0, 0], weight_ref[...]).astype(BF16)
    for position, ref in enumerate(out_refs):

        @pl.when(piece == position)
        def _():
            ref[0] = result


def spread_back(grad_qkv, weights, *earlier):
    pieces, rows, frames, triple = grad_qkv.shape
    model = weights.shape[0]

    def out_spec(position):
        return pl.BlockSpec(
            (1, frames, model),
            lambda m, r: (jnp.where(m < position, 0, jnp.where(m == position, r, rows - 1)), 0, 0),
        )

    return pl.pallas_call(
        functools.partial(spread_back_kernel, pieces - 1),
        grid=(pieces - 1, rows),
        out_shape=(jax.ShapeDtypeStruct((rows, frames, model), BF16),) * (pieces - 1),
        in_specs=[
            pl.BlockSpec((1, 1, frames, triple), lambda m, r: (m + 1, r, 0, 0)),
            pl.BlockSpec(weights.shape, lambda m, r: (0, 0)),
        ]
        + [ANY_SPEC] * len(earlier),
        out_specs=tuple(out_spec(position) for position in range(pieces - 1)),
        compiler_params=pltpu.CompilerParams(vmem_limit_bytes=VMEM_LIMIT),
        cost_estimate=pl.CostEstimate(
            flops=2 * (pieces - 1) * rows * frames * triple * model,
            bytes_accessed=2 * pieces * rows * frames * (triple + model),
            transcendentals=0,
        ),
        name="spread_back",
    )(grad_qkv, weights, *earlier)


def head_lanes(shape, heads, width, split):
    lane = lax.broadcasted_iota(jnp.int32, shape, 1)
    size = width // heads
    if split:
        return (lane % (width // 2)) // (size // 2)
    return lane // size


def column_of(row, lanes):
    return jnp.broadcast_to(row, (128, row.shape[1])).T[:, :lanes]


def attend_kernel(heads, width, qkv_ref, seg_ref, *rest):
    pieces, _, frames, _ = qkv_ref.shape
    out_refs, (lse_ref, vt_ref, ot_ref, seg_col_ref) = rest[:pieces], rest[pieces:]
    length = pieces * frames
    step = pl.program_id(1)
    size = width // heads
    keys = qkv_ref[:, 0, :, width : 2 * width].reshape(length, width)

    @pl.when(step == 0)
    def _():
        vt_ref[...] = qkv_ref[:, 0, :, 2 * width :].reshape(length, width).T
        for piece in range(pieces):
            seg_col_ref[piece * frames : (piece + 1) * frames, :] = column_of(seg_ref[0, piece : piece + 1, :], 128)

    queries = qkv_ref[step, 0, :, :width]
    owner = head_lanes((frames, width), heads, width, True)
    allowed = seg_col_ref[:, :1] == seg_ref[0, pl.ds(step, 1), :]
    for head in range(heads):
        masked = jnp.where(owner == head, queries, jnp.zeros_like(queries))
        scores = jnp.where(allowed, against(keys, masked), MASKED)
        highest = jnp.max(scores, 0, keepdims=True)
        raised = jnp.exp(scores - highest)
        total = jnp.sum(raised, 0, keepdims=True)
        lse_ref[0, 0, head : head + 1, :] = highest + jnp.log(total)
        result = dot(vt_ref[head * size : (head + 1) * size, :], raised.astype(BF16))
        ot_ref[head * size : (head + 1) * size, :] = result / total
    result = ot_ref[...].T.astype(BF16)
    for piece in range(pieces):

        @pl.when(step == piece)
        def _():
            out_refs[piece][0] = result


def attend(qkv, seg, row, heads):
    pieces, rows, frames, triple = qkv.shape
    width = triple // 3
    length = pieces * frames
    results = pl.pallas_call(
        functools.partial(attend_kernel, heads, width),
        grid=(rows, pieces),
        out_shape=(jax.ShapeDtypeStruct((rows, frames, width), BF16),) * pieces
        + (jax.ShapeDtypeStruct((rows, pieces, heads, frames), F32),),
        in_specs=[
            pl.BlockSpec((pieces, 1, frames, triple), lambda r, s: (0, r, 0, 0)),
            pl.BlockSpec((1, pieces, frames), lambda r, s: (row, 0, 0)),
        ],
        out_specs=(pl.BlockSpec((1, frames, width), lambda r, s: (r, 0, 0)),) * pieces
        + (pl.BlockSpec((1, 1, heads, frames), lambda r, s: (r, s, 0, 0)),),
        scratch_shapes=[
            pltpu.VMEM((width, length), BF16),
            pltpu.VMEM((width, frames), F32),
            pltpu.VMEM((length, 128), F32),
        ],
        compiler_params=pltpu.CompilerParams(vmem_limit_bytes=VMEM_LIMIT),
        cost_estimate=pl.CostEstimate(
            flops=4 * rows * length * length * 256 * heads,
            bytes_accessed=8 * rows * length * width,
            transcendentals=rows * heads * length * length,
        ),
        name="attend",
    )(qkv, seg)
    return results[:pieces], results[pieces]


def attend_back_kernel(heads, width, scale, qkv_ref, seg_ref, lse_ref, cos_ref, sin_ref, *rest):
    pieces, _, frames, _ = qkv_ref.shape
    out_refs, grad_refs = rest[:pieces], rest[pieces : 2 * pieces]
    result_ref, kt_ref, dk_ref, dv_ref, dqt_ref, seg_col_ref, out_ref, grad_ref = rest[-8:]
    length = pieces * frames
    step = pl.program_id(1)
    size, half = width // heads, width // 2
    keys = qkv_ref[:, 0, :, width : 2 * width].reshape(length, width)
    values = qkv_ref[:, 0, :, 2 * width :].reshape(length, width)

    @pl.when(step == 0)
    def _():
        kt_ref[...] = keys.T
        dk_ref[...] = jnp.zeros_like(dk_ref)
        dv_ref[...] = jnp.zeros_like(dv_ref)
        for piece in range(pieces):
            seg_col_ref[piece * frames : (piece + 1) * frames, :] = column_of(seg_ref[0, piece : piece + 1, :], 128)
            out_ref[piece] = out_refs[piece][0]
            grad_ref[piece] = grad_refs[piece][0]

    queries = qkv_ref[step, 0, :, :width]
    grad = grad_ref[step]
    query_owner = head_lanes((frames, width), heads, width, True)
    value_owner = head_lanes((frames, width), heads, width, False)
    allowed = seg_col_ref[:, :1] == seg_ref[0, pl.ds(step, 1), :]
    product = grad.astype(F32) * out_ref[step].astype(F32)
    picker = lax.broadcasted_iota(jnp.int32, (8, width), 1) // size == lax.broadcasted_iota(jnp.int32, (8, width), 0)
    inner = lax.dot_general(
        picker.astype(F32), product, NT, precision=lax.Precision.HIGHEST, preferred_element_type=F32
    )
    for head in range(heads):
        masked = jnp.where(query_owner == head, queries, jnp.zeros_like(queries))
        masked_grad = jnp.where(value_owner == head, grad, jnp.zeros_like(grad))
        scores = against(keys, masked)
        weights = jnp.where(allowed, jnp.exp(scores - lse_ref[0, 0, head : head + 1, :]), 0.0)
        grad_weights = against(values, masked_grad)
        grad_scores = (weights * (grad_weights - inner[head : head + 1, :])).astype(BF16)
        dv_ref[...] += dot(weights.astype(BF16), masked_grad)
        dk_ref[...] += dot(grad_scores, masked)
        low, high = head * size // 2, half + head * size // 2
        head_keys = jnp.concatenate([kt_ref[low : low + size // 2, :], kt_ref[high : high + size // 2, :]], 0)
        part = dot(head_keys, grad_scores)
        dqt_ref[low : low + size // 2, :] = part[: size // 2]
        dqt_ref[high : high + size // 2, :] = part[size // 2 :]

    def unrotate(values, cosine, sine):
        low, high = values[:, :half], values[:, half:]
        return (low * cosine + high * sine).astype(BF16), (high * cosine - low * sine).astype(BF16)

    low, high = unrotate(dqt_ref[...].T * scale, cos_ref[step], sin_ref[step])
    result_ref[step, 0, :, :half] = low
    result_ref[step, 0, :, half:width] = high

    @pl.when(step == pieces - 1)
    def _():
        for piece in range(pieces):
            span = slice(piece * frames, (piece + 1) * frames)
            low, high = unrotate(dk_ref[span, :], cos_ref[piece], sin_ref[piece])
            result_ref[piece, 0, :, width : width + half] = low
            result_ref[piece, 0, :, width + half : 2 * width] = high
            result_ref[piece, 0, :, 2 * width :] = dv_ref[span, :].astype(BF16)


def attend_back(qkv, seg, row, lse, cos_table, sin_table, outs, grads, heads, scale, earlier):
    pieces, rows, frames, triple = qkv.shape
    width = triple // 3
    length = pieces * frames
    whole = pl.BlockSpec((pieces, 1, frames, triple), lambda r, s: (0, r, 0, 0))
    table = pl.BlockSpec((pieces, frames, width // 2), lambda r, s: (0, 0, 0))
    block = pl.BlockSpec((1, frames, width), lambda r, s: (r, 0, 0))
    return pl.pallas_call(
        functools.partial(attend_back_kernel, heads, width, scale),
        grid=(rows, pieces),
        out_shape=jax.ShapeDtypeStruct(qkv.shape, BF16),
        in_specs=[
            whole,
            pl.BlockSpec((1, pieces, frames), lambda r, s: (row, 0, 0)),
            pl.BlockSpec((1, 1, heads, frames), lambda r, s: (r, s, 0, 0)),
            table,
            table,
        ]
        + [block] * (2 * pieces)
        + [ANY_SPEC] * len(earlier),
        out_specs=whole,
        scratch_shapes=[
            pltpu.VMEM((width, length), BF16),
            pltpu.VMEM((length, width), F32),
            pltpu.VMEM((length, width), F32),
            pltpu.VMEM((width, frames), F32),
            pltpu.VMEM((length, 128), F32),
            pltpu.VMEM((pieces, frames, width), BF16),
            pltpu.VMEM((pieces, frames, width), BF16),
        ],
        compiler_params=pltpu.CompilerParams(vmem_limit_bytes=VMEM_LIMIT),
        cost_estimate=pl.CostEstimate(
            flops=10 * rows * length * length * 256 * heads,
            bytes_accessed=16 * rows * length * width,
            transcendentals=rows * heads * length * length,
        ),
        name="attend_back",
    )(qkv, seg, lse, cos_table, sin_table, *outs, *grads, *earlier)


def mlp_kernel(bank, chunk, place_ref, normed_ref, grad_ref, bank_ref, *rest):
    fed_ref, gn_ref, grads_ref, nt_ref, gt_ref, weight_ref, result_ref, sems = rest
    step, rows = pl.program_id(0), bank.rows
    units = bank.columns // 2
    per_place = units // chunk
    half = bank.arrays[0].shape[0]

    def copies(block, slot):
        start = (block % per_place) * chunk
        target, found = weight_ref.at[slot], []
        for which in range(2):
            found += bank_copies(
                bank, bank_ref, block // per_place, which * units + start, chunk, target,
                sems.at[slot, pl.ds(which * half, half)], which * chunk,
            )
        return found

    @pl.when(step == 0)
    def _():
        for copy in copies(0, 0):
            copy.start()
        nt_ref[...] = normed_ref[...].T
        gt_ref[...] = grad_ref[...].T
        fed_ref[...] = jnp.zeros_like(fed_ref)
        gn_ref[...] = jnp.zeros_like(gn_ref)

    for block in range(1, axis_size("seq") * per_place):

        @pl.when(step + 1 == block)
        def _():
            for copy in copies(block, block % 2):
                copy.start()

    slot = step % 2
    for copy in copies(0, slot):
        copy.wait()
    up, down = weight_ref[slot, :, :chunk], weight_ref[slot, :, chunk:]
    before = dot(normed_ref[...], up)
    square = before * before
    factor = math.sqrt(2.0 / math.pi)
    bent = jnp.tanh(factor * (before + 0.044715 * (square * before)))
    activated = (0.5 * before * (1.0 + bent)).astype(BF16)
    slope = 0.5 * (1.0 + bent) + 0.5 * before * (1.0 - bent * bent) * (factor * (1.0 + 3 * 0.044715 * square))
    grad_before = (dot(grad_ref[...], down) * slope).astype(BF16)
    fed_ref[...] += against(activated, down)
    gn_ref[...] += against(grad_before, up)
    result_ref[:, :chunk] = dot(nt_ref[...], grad_before).astype(BF16)
    result_ref[:, chunk:] = dot(gt_ref[...], activated).astype(BF16)
    for owner in range(grads_ref.shape[0]):
        grads_ref[owner, 0] = result_ref[owner * rows : (owner + 1) * rows, :]


def mlp(place, normed, grad, bank):
    tokens, model = normed.shape
    seqs, owners = axis_size("seq"), axis_size("dp")
    units = bank.columns // 2
    chunk = min(512, units)
    per_place = units // chunk
    whole = pl.BlockSpec((tokens, model), lambda i: (0, 0))
    hidden = seqs * units
    return pl.pallas_call(
        functools.partial(mlp_kernel, bank, chunk),
        grid=(seqs * per_place,),
        out_shape=(jax.ShapeDtypeStruct((tokens, model), F32),) * 2
        + (jax.ShapeDtypeStruct((owners, seqs, bank.rows, 2 * units), BF16),),
        in_specs=[SMEM_SPEC, whole, whole, ANY_SPEC],
        out_specs=(
            whole,
            whole,
            pl.BlockSpec((owners, 1, bank.rows, 2 * chunk), lambda i: (0, i // per_place, 0, i % per_place)),
        ),
        scratch_shapes=[
            pltpu.VMEM((model, tokens), BF16),
            pltpu.VMEM((model, tokens), BF16),
            pltpu.VMEM((2, model, 2 * chunk), BF16),
            pltpu.VMEM((model, 2 * chunk), BF16),
            pltpu.SemaphoreType.DMA((2, 2 * owners)),
        ],
        compiler_params=pltpu.CompilerParams(vmem_limit_bytes=VMEM_LIMIT),
        cost_estimate=pl.CostEstimate(
            flops=12 * tokens * model * hidden,
            bytes_accessed=8 * model * hidden + 12 * tokens * model,
            transcendentals=tokens * hidden,
        ),
        name="mlp",
    )(place, normed, grad, *bank.arrays)


def standardize(values):
    centre = values - jnp.mean(values, -1, keepdims=True)
    inverse = lax.rsqrt(jnp.mean(centre * centre, -1, keepdims=True) + EPSILON)
    return centre * inverse, inverse


def standardize_back(grad, standard, inverse):
    return inverse * (
        grad - jnp.mean(grad, -1, keepdims=True) - standard * jnp.mean(grad * standard, -1, keepdims=True)
    )


def utterance_of(seg_ref):
    return column_of(seg_ref[0], 1)


def by_frame(owner, mod_ref, part):
    count = mod_ref.shape[1]
    result = mod_ref[0, count - 1, part : part + 1, :]
    for position in range(count - 2, -1, -1):
        result = jnp.where(owner == float(position), mod_ref[0, position, part : part + 1, :], result)
    return result


def add_up(owner, values, out_ref, part, count):
    for position in range(count):
        out_ref[0, part, position : position + 1, :] = jnp.sum(
            jnp.where(owner == float(position), values, 0.0), 0, keepdims=True
        )


def start_weight(pieces, refs, target, sems, place_ref, relative):
    copies = weight_copies(pieces, refs, target, sems, place_ref, relative)
    for copy in copies:
        copy.start()
    return copies


def wait_all(copies):
    for copy in copies:
        copy.wait()


def row_call(kernel, name, place, row, by_row, fixed, pieces, weight_shape, outs, held, flops, earlier=()):
    row_spec = lambda shape: pl.BlockSpec(
        (1,) + tuple(shape[1:]), lambda i: (row if shape[0] > 1 else 0,) + (0,) * (len(shape) - 1)
    )
    fixed_specs = [pl.BlockSpec(array.shape, lambda i, n=array.ndim: (0,) * n) for array in fixed]
    size = sum(array.size * array.dtype.itemsize for array in by_row) + 2 * math.prod(weight_shape)
    first = len(place) + len(by_row) + len(fixed) + len(pieces.arrays)
    kept = [position for position, out in enumerate(outs) if held and out.shape[0] > 1]
    held = [held[position] for position in kept]
    aliases = {first + number: position for number, position in enumerate(kept)}
    return pl.pallas_call(
        kernel,
        grid=(1,),
        out_shape=tuple(outs),
        in_specs=[SMEM_SPEC] * len(place)
        + [row_spec(array.shape) for array in by_row]
        + fixed_specs
        + [ANY_SPEC] * (len(pieces.arrays) + len(held) + len(earlier)),
        out_specs=tuple(row_spec(out.shape) for out in outs),
        input_output_aliases=aliases,
        scratch_shapes=[pltpu.VMEM(weight_shape, BF16), pltpu.SemaphoreType.DMA((copy_count(pieces),))],
        compiler_params=pltpu.CompilerParams(vmem_limit_bytes=VMEM_LIMIT),
        cost_estimate=pl.CostEstimate(flops=flops, bytes_accessed=size, transcendentals=0),
        name=name,
    )(*place, *by_row, *fixed, *pieces.arrays, *held, *earlier)


def enter_kernel(pieces, row, place_ref, coef_ref, frames_ref, skip_ref, cond_ref, seg_ref, mod_ref, *rest):
    refs, (hidden_ref, normed_ref, weight_ref, sems) = rest[: len(pieces.arrays)], rest[-4:]
    copies = start_weight(pieces, refs, weight_ref, sems, place_ref, False)
    model = frames_ref.shape[2]
    owner = utterance_of(seg_ref)
    count = mod_ref.shape[1]
    factor = coef_ref[row, count - 1]
    for position in range(count - 2, -1, -1):
        factor = jnp.where(owner == float(position), coef_ref[row, position], factor)
    wait_all(copies)
    hidden = dot(frames_ref[0], weight_ref[:model, :]) + dot(skip_ref[0], weight_ref[model:, :])
    hidden = hidden + factor * cond_ref[0].astype(F32)
    hidden_ref[0] = hidden
    standard, _ = standardize(hidden)
    normed_ref[0] = (standard * (1.0 + by_frame(owner, mod_ref, 1)) + by_frame(owner, mod_ref, 0)).astype(BF16)


def branch_kernel(pieces, count, place_ref, *rest):
    blocks, (hidden_ref, cot_ref, seg_ref, mod_ref) = rest[:count], rest[count : count + 4]
    refs = rest[count + 4 : count + 4 + len(pieces.arrays)]
    attn_ref, branch_ref, middle_ref, normed_ref, grad_ref, weight_ref, sems = rest[-7:]
    copies = start_weight(pieces, refs, weight_ref, sems, place_ref, True)
    owner = utterance_of(seg_ref)
    attn = jnp.concatenate([block[0] for block in blocks], -1)
    attn_ref[0] = attn
    wait_all(copies)
    branch = against(attn, weight_ref[...])
    branch_ref[0] = branch
    middle = hidden_ref[0] + by_frame(owner, mod_ref, 2) * branch
    middle_ref[0] = middle
    standard, _ = standardize(middle)
    normed_ref[0] = (standard * (1.0 + by_frame(owner, mod_ref, 4)) + by_frame(owner, mod_ref, 3)).astype(BF16)
    grad_ref[0] = (by_frame(owner, mod_ref, 5) * cot_ref[0].astype(F32)).astype(BF16)


def middle_back_kernel(pieces, seqs, place_ref, middle_ref, fed_ref, gn_ref, cot_ref, branch_ref, seg_ref, mod_ref, *rest):
    refs = rest[: len(pieces.arrays)]
    output_ref, grad_ref, grad_branch_ref, sums_ref = rest[-6 - seqs : -2 - seqs]
    block_refs, (weight_ref, sems) = rest[-2 - seqs : -2], rest[-2:]
    copies = start_weight(pieces, refs, weight_ref, sems, place_ref, True)
    owner, count = utterance_of(seg_ref), mod_ref.shape[1]
    middle, fed, grad_norm, grad_out = middle_ref[0], fed_ref[0], gn_ref[0], cot_ref[0].astype(F32)
    output_ref[0] = (middle + by_frame(owner, mod_ref, 5) * fed).astype(BF16)
    standard, inverse = standardize(middle)
    grad_middle = grad_out + standardize_back(grad_norm * (1.0 + by_frame(owner, mod_ref, 4)), standard, inverse)
    grad_ref[0] = grad_middle
    grad_branch = (by_frame(owner, mod_ref, 2) * grad_middle).astype(BF16)
    grad_branch_ref[0] = grad_branch
    wait_all(copies)
    grad_attn = dot(grad_branch, weight_ref[...]).astype(BF16)
    width = grad_attn.shape[1] // seqs
    for seq in range(seqs):
        block_refs[seq][0] = grad_attn[:, seq * width : (seq + 1) * width]
    add_up(owner, grad_middle * branch_ref[0], sums_ref, 0, count)
    add_up(owner, grad_norm, sums_ref, 1, count)
    add_up(owner, grad_norm * standard, sums_ref, 2, count)
    add_up(owner, grad_out * fed, sums_ref, 3, count)


def leave_kernel(pieces, seqs, place_ref, hidden_ref, grad_middle_ref, own_ref, *rest):
    got = rest[: seqs - 1]
    seg_ref, mod_ref, qkv_ref = rest[seqs - 1 : seqs + 2]
    refs = rest[seqs + 2 : seqs + 2 + len(pieces.arrays)]
    columns_ref, frames_ref, skip_ref, sums_ref, weight_ref, sems = rest[-6:]
    copies = start_weight(pieces, refs, weight_ref, sems, place_ref, False)
    owner, count = utterance_of(seg_ref), mod_ref.shape[1]
    grad_norm = against(own_ref[0], qkv_ref[...])
    for ref in got:
        grad_norm = grad_norm + ref[0].astype(F32)
    standard, inverse = standardize(hidden_ref[0])
    grad = standardize_back(grad_norm * (1.0 + by_frame(owner, mod_ref, 1)), standard, inverse)
    grad_hidden = (grad_middle_ref[0] + grad).astype(BF16)
    model = grad_hidden.shape[1]
    wait_all(copies)
    frames_ref[0] = against(grad_hidden, weight_ref[:model, :]).astype(BF16)
    skip_ref[0] = against(grad_hidden, weight_ref[model:, :]).astype(BF16)
    add_up(owner, grad_norm, sums_ref, 0, count)
    add_up(owner, grad_norm * standard, sums_ref, 1, count)
    width = model // seqs
    turned = grad_hidden.astype(F32)
    bit = 1
    while bit < seqs:
        parts = [turned[:, (s ^ bit) * width : ((s ^ bit) + 1) * width] for s in range(seqs)]
        turned = jnp.where((place_ref[1] // bit) % 2 == 1, jnp.concatenate(parts, -1), turned)
        bit *= 2
    columns_ref[0] = turned.astype(BF16)


def time_embed(flow_values, model_width):
    half_dim = model_width // 2
    frequency = jnp.exp(jnp.arange(half_dim, dtype=F32) * (-math.log(10000.0) / half_dim))
    angles = 1000.0 * flow_values[..., None] * frequency
    return jnp.concatenate([jnp.sin(angles), jnp.cos(angles)], -1)


def body(
    frames, skip_in, cond, seg_ids, drop_flags, flow_times, w_skip, w_qkv, w_out, w_up, w_down, w_mod, cotangent
):
    row_count, frame_count, model = frames.shape
    seq_size, dp_size = axis_size("seq"), axis_size("dp")
    chips = dp_size // CORES
    dp, seq = lax.axis_index(AXES["dp"]), lax.axis_index(AXES["seq"])
    place = jnp.stack([dp, seq]).astype(jnp.int32)
    head_dim = model // HEADS
    heads = HEADS // seq_size
    width = heads * head_dim
    half = head_dim // 2
    scale = head_dim ** (-0.5)
    tokens = row_count * frame_count
    segs = drop_flags.shape[1]
    frame_shape = (row_count, frame_count, model)
    partners = range(1, seq_size)
    fast, slow = seq_halves()
    rows = w_up.shape[0]
    shape_of = jax.ShapeDtypeStruct

    by_head = w_qkv.reshape(w_qkv.shape[0], heads, 3, 2, half)
    qkv_shard = jnp.concatenate(
        [
            by_head[:, :, 0].swapaxes(1, 2).reshape(-1, width),
            by_head[:, :, 1].swapaxes(1, 2).reshape(-1, width),
            by_head[:, :, 2].reshape(-1, width),
        ],
        1,
    )
    skip_parts = pack(gather_over(start_gather(w_skip), "dp", chip_masks()))

    skip_near = skip_parts.arrays[0]

    small = jnp.concatenate([flow_times, drop_flags.astype(F32)], 1)
    small = gather_steps(small, [("dp", chip_masks())])
    mod_rows, mod_columns = w_mod.shape
    mod_pair = swap(w_mod, "dp", 1)
    utterances = row_count * segs

    def activity_of(values, owner):
        result = jax.nn.silu(time_embed(values, model)).astype(BF16).reshape(-1, model)
        return lax.dynamic_slice_in_dim(result, owner * mod_rows, mod_rows, 1)

    modulation = dot(activity_of(small[..., :segs], dp), w_mod)
    modulation = modulation + dot(activity_of(small[..., :segs], dp ^ 1), mod_pair)
    modulation = modulation.reshape(chips, utterances, mod_columns)
    for mask in reversed(bits("dp")):
        count = modulation.shape[0] // 2
        modulation = modulation[:count] + swap(modulation[count:], "dp", mask)
    modulation = modulation[0]

    small = jnp.stack([small, swap(small, "dp", 1)])
    dropped = jnp.sum(small[..., segs:])
    slots = float(row_count * segs * dp_size)
    cond_scale = slots / jnp.maximum(slots - dropped, 1.0)
    coefficients = (1.0 - drop_flags.astype(F32)) * cond_scale

    if narrow(w_skip):
        skip_parts = whole_columns(w_skip, place, False)
        arrived = skip_parts.arrays[0]
    else:
        skip_parts = gather_over(skip_parts, "seq", partners)
        arrived = skip_parts.arrays[-1]
        skip_parts = gather_over(skip_parts, "dp", [1])

    extra = -(-tokens // mod_columns)
    numbers = jnp.pad(seg_ids.astype(F32).reshape(-1), (0, extra * mod_columns - tokens)).reshape(extra, mod_columns)
    own_mod = jnp.concatenate([modulation, numbers])
    all_mod = jnp.stack([own_mod] + [swap(own_mod, "seq", mask) for mask in partners])
    segments = all_mod[:, utterances:].reshape(seq_size, -1)[:, :tokens].reshape(seq_size, row_count, frame_count)
    segments = segments.swapaxes(0, 1)
    modulation = jnp.take(all_mod[:, :utterances], jnp.arange(seq_size) ^ seq, axis=0)
    modulation = modulation.swapaxes(0, 1).reshape(row_count, segs, 6, model)
    seg_here = segments[:, :1]

    qkv_parts = start_gather(qkv_shard)
    for mask in bits("dp"):
        qkv_parts = pack(gather_over(qkv_parts, "dp", [mask]))
    qkv_full = assemble(gather_over(qkv_parts, "dp", [1]), place, (dp_size * rows, 3 * width))

    units = w_up.shape[1]
    bank = pack_bank([arrived, all_mod, qkv_parts.arrays[0]], w_up, w_down)
    bank = lax.all_gather(bank, AXES["all"], axis=0)
    bank = Bank(bank.reshape((dp_size, seq_size) + bank.shape[1:]), 0, 2 * units)

    row_range = range(row_count)
    one_row = (1,) + frame_shape[1:]
    entered, normed = None, []
    for row in row_range:
        entered = row_call(
            functools.partial(enter_kernel, skip_parts, row),
            "enter",
            [place, coefficients],
            row,
            [frames, skip_in, cond, seg_here, modulation],
            [],
            skip_parts,
            (2 * model, model),
            [shape_of(frame_shape, F32), shape_of(one_row, BF16)],
            entered,
            4 * frame_count * model * model,
        )
        normed.append(entered[1])
    hidden = entered[0]

    positions = (jnp.arange(seq_size) ^ seq)[:, None] * frame_count + jnp.arange(frame_count)
    frequency = jnp.exp((jnp.arange(width // 2) % half).astype(F32) * (-2.0 * math.log(10000.0) / head_dim))
    angles = positions.astype(F32)[..., None] * frequency
    cos_table, sin_table = jnp.cos(angles), jnp.sin(angles)

    pieces = [[normed[row]] + [swap(normed[row], "seq", mask) for mask in partners] for row in row_range]
    if narrow(w_out.T):
        out_parts = whole_columns(w_out.T, place, True)
    else:
        out_parts = pack(gather_over(start_gather(after(w_out.T, pieces[0][-1])), "dp", chip_masks()))
        out_parts = gather_over(gather_over(out_parts, "seq", partners), "dp", [1])
    qkv, attended, lse, branched = [], [], [], None
    for row in row_range:
        qkv.append(project(pieces[row], qkv_full, cos_table, sin_table, scale))
        result = attend(qkv[row], segments, row, heads)
        attended.append(result[0])
        lse.append(result[1])
    for row in row_range:
        blocks = [attended[row][0]] + [swap(attended[row][mask], "seq", mask) for mask in partners]
        branched = row_call(
            functools.partial(branch_kernel, out_parts, seq_size),
            "branch",
            [place],
            row,
            blocks + [hidden, cotangent, seg_here, modulation],
            [],
            out_parts,
            (model, model),
            [shape_of(frame_shape, dtype) for dtype in (BF16, F32, F32, BF16, BF16)],
            branched,
            2 * frame_count * model * model,
        )
    attn, branch, middle, normed_two, grad_fed = branched
    fed, grad_norm_two, grad_bank = mlp(
        place, normed_two.reshape(tokens, model), grad_fed.reshape(tokens, model), bank
    )
    sum_bank = lax.psum_scatter(grad_bank, AXES["dp"], scatter_dimension=0, tiled=True)[0]
    fed, grad_norm_two = fed.reshape(frame_shape), grad_norm_two.reshape(frame_shape)
    returned, grad_heads, sums_two = None, [], []
    for row in row_range:
        returned = row_call(
            functools.partial(middle_back_kernel, out_parts, seq_size),
            "middle_back",
            [place],
            row,
            [middle, fed, grad_norm_two, cotangent, branch, seg_here, modulation],
            [],
            out_parts,
            (model, model),
            [
                shape_of(frame_shape, BF16),
                shape_of(frame_shape, F32),
                shape_of(frame_shape, BF16),
                shape_of((1, 4, 8, model), F32),
            ]
            + [shape_of((1, frame_count, width), BF16)] * seq_size,
            returned,
            2 * frame_count * model * model,
        )
        sums_two.append(returned[3])
        grad_heads.append([returned[4]] + [swap(returned[4 + mask], "seq", mask) for mask in partners])
    output, grad_middle, grad_branch = returned[:3]
    keep_out, give_out = weight_grad(
        place, [grad_branch.reshape(tokens, model)], [attn.reshape(tokens, model)], True, rows, seq_size, False
    )
    sum_out, _ = send_seq(add_cores(keep_out, give_out))

    grad_qkv, got, partials = [], [], []
    for row in row_range:
        grad_qkv.append(
            attend_back(
                qkv[row], segments, row, lse[row], cos_table, sin_table, attended[row], grad_heads[row], heads, scale,
                partials,
            )
        )
        earlier = [sum_out] if row == row_count - 1 else []
        partials = spread_back(grad_qkv[row], qkv_full, *earlier)
        got.append([swap(partial, "seq", mask) for mask, partial in zip(partners, partials)])
    keep_qkv, give_qkv = weight_grad(
        place,
        [piece.reshape(frame_count, model) for row_pieces in pieces for piece in row_pieces],
        grad_qkv,
        True,
        rows,
        1,
        False,
        got[0][-1],
    )
    sum_pair = jnp.concatenate([sum_out, add_cores(keep_qkv, give_qkv)[0]], -1).astype(BF16)
    sum_pair = after(sum_pair, sum_bank)
    sum_pair = after(lax.psum_scatter(sum_pair, "chip", scatter_dimension=0, tiled=True)[0]).astype(F32)

    left, sums_one = None, []
    for row in row_range:
        left = row_call(
            functools.partial(leave_kernel, skip_parts, seq_size),
            "leave",
            [place],
            row,
            [hidden, grad_middle, grad_qkv[row][0]] + got[row] + [seg_here, modulation],
            [qkv_full],
            skip_parts,
            (2 * model, model),
            [shape_of(frame_shape, BF16)] * 3 + [shape_of((1, 2, 8, model), F32)],
            left,
            6 * frame_count * model * model,
            [keep_qkv] if row == 0 else [],
        )
        sums_one.append(left[3])
    grad_columns, grad_frames, grad_skip = left[:3]
    sums_one, sums_two = jnp.concatenate(sums_one), jnp.concatenate(sums_two)
    grad_modulation = jnp.concatenate([sums_one, sums_two], 1)[:, :, :segs]
    grad_modulation = grad_modulation.swapaxes(1, 2).reshape(utterances, 6 * model)
    own = lax.dynamic_slice_in_dim(grad_modulation, seq * mod_columns, mod_columns, 1)
    for mask in partners:
        own = own + swap(
            lax.dynamic_slice_in_dim(grad_modulation, (seq ^ mask) * mod_columns, mod_columns, 1), "seq", mask
        )
    keep_skip, give_skip = weight_grad(
        place,
        [frames.reshape(tokens, model), skip_in.reshape(tokens, model)],
        [grad_columns.reshape(tokens, model)],
        False,
        w_skip.shape[0],
        seq_size,
        True,
        own,
    )
    sum_skip, _ = send_seq(add_cores(keep_skip, give_skip))

    wide = pick(sum_bank, seq, 0).astype(F32)
    for mask in partners:
        wide = wide + swap(pick(sum_bank, seq ^ mask, 0), "seq", mask).astype(F32)
    sum_up, sum_down = unpack_sums(wide, units, min(512, units))
    skip_shard = send_chips(sum_skip)
    sum_out, sum_qkv = sum_pair[:, :width].T, sum_pair[:, width:]
    sum_qkv = jnp.stack(
        [
            sum_qkv[:, :width].reshape(rows, 2, heads, half).swapaxes(1, 2).reshape(rows, heads, head_dim),
            sum_qkv[:, width : 2 * width].reshape(rows, 2, heads, half).swapaxes(1, 2).reshape(rows, heads, head_dim),
            sum_qkv[:, 2 * width :].reshape(rows, heads, head_dim),
        ],
        2,
    ).reshape(rows, 3 * width)

    own = gather_steps(own, [("dp", chip_masks()), ("dp", [1])]).reshape(dp_size * utterances, mod_columns)
    activity = activity_of(small[..., :segs], dp)
    sum_mod = jnp.dot(activity.astype(F32).T, own, precision=lax.Precision.HIGHEST)
    return (
        output,
        grad_frames,
        grad_skip,
        skip_shard,
        sum_qkv,
        sum_out,
        sum_up,
        sum_down,
        sum_mod,
    )


def solution(mesh):
    chips, seqs = mesh.shape["dp"] // CORES, mesh.shape["seq"]
    fast = 1
    while fast * fast < seqs:
        fast *= 2
    cut = Mesh(mesh.devices.reshape(chips, CORES, seqs // fast, fast), ("chip", "core", "slow", "fast"))
    dp, seq = AXES["dp"], AXES["seq"]
    tokens, rows, both, turned = P(dp, seq, None), P(dp, None), P(dp, seq), P(seq, dp)
    in_specs = (tokens, tokens, tokens, both, rows, rows, both, both, turned, both, turned, both, tokens)
    out_specs = (tokens, tokens, tokens, both, both, turned, both, turned, both)
    return jax.shard_map(body, mesh=cut, in_specs=in_specs, out_specs=out_specs, check_vma=False)
```

```python
import functools
import math

import jax
import jax.numpy as jnp
from jax import lax
from jax.experimental import pallas as pl
from jax.experimental.pallas import tpu as pltpu
from jax.sharding import Mesh
from jax.sharding import PartitionSpec as P

HEADS = 16
AXES = {"dp": ("chip", "core"), "seq": ("slow", "fast"), "all": ("chip", "core", "slow", "fast")}
CORES = 2
EPSILON = 1e-06
MASKED = -1e30
VMEM_LIMIT = 60 * 1024 * 1024
F32 = jnp.float32
BF16 = jnp.bfloat16
NT = (((1,), (1,)), ((), ()))
TN = (((0,), (0,)), ((), ()))


def dot(left, right):
    return jnp.dot(left, right, preferred_element_type=F32)


def against(left, right):
    return lax.dot_general(left, right, NT, preferred_element_type=F32)


def over_rows(left, right):
    return lax.dot_general(left, right, TN, preferred_element_type=F32)


def axis_size(axis):
    return math.prod(lax.axis_size(name) for name in AXES[axis])


def swap(values, axis, mask):
    return lax.ppermute(values, AXES[axis], [(i, i ^ mask) for i in range(axis_size(axis))])


def chip_masks():
    return [CORES * k for k in range(1, axis_size("dp") // CORES)]


def bits(axis):
    found, mask = [], CORES if axis == "dp" else 1
    while mask < axis_size(axis):
        found.append(mask)
        mask *= 2
    return found


def seq_halves():
    fast, slow = lax.axis_size("fast"), lax.axis_size("slow")
    return [list(range(1, fast)), [fast * k for k in range(1, slow)]]


def gather_steps(shard, steps):
    held = shard
    for axis, masks in steps:
        held = jnp.stack([held] + [swap(held, axis, mask) for mask in masks])
    return held


SMEM_SPEC = pl.BlockSpec(memory_space=pltpu.SMEM)
ANY_SPEC = pl.BlockSpec(memory_space=pl.ANY)


def pass_kernel(*refs):
    del refs


def after(value, *earlier):
    return pl.pallas_call(
        pass_kernel,
        out_shape=jax.ShapeDtypeStruct(value.shape, value.dtype),
        in_specs=[ANY_SPEC] * (1 + len(earlier)),
        out_specs=ANY_SPEC,
        input_output_aliases={0: 0},
        name="after",
    )(value, *earlier)


class Pieces:
    def __init__(self, arrays, masks, rows, columns):
        self.arrays, self.masks, self.rows, self.columns = arrays, masks, rows, columns


def start_gather(shard):
    return Pieces([shard[None]], [[(0, 0)]], *shard.shape)


def gather_over(held, axis, masks):
    arrays, tables = list(held.arrays), list(held.masks)
    for mask in masks:
        for array, table in zip(held.arrays, held.masks):
            arrays.append(swap(array, axis, mask))
            tables.append([(d ^ mask, s) if axis == "dp" else (d, s ^ mask) for d, s in table])
    return Pieces(arrays, tables, held.rows, held.columns)


def pack(held):
    if len(held.arrays) == 1:
        return held
    return Pieces(
        [jnp.concatenate(held.arrays)], [[entry for table in held.masks for entry in table]], held.rows, held.columns
    )


def hold(held, *earlier):
    return Pieces([after(array, *earlier) for array in held.arrays], held.masks, held.rows, held.columns)


def gather_seq(held, masks):
    held = gather_over(held, "seq", masks)
    return pack(held) if axis_size("seq") > 4 else held


def whole_columns(shard, place, relative):
    held = lax.all_gather(lax.all_gather(shard, AXES["dp"], axis=0, tiled=True), AXES["seq"], axis=0)
    if relative:
        held = jnp.take(held, jnp.arange(held.shape[0]) ^ place[1], axis=0)
    full = jnp.moveaxis(held, 0, 1).reshape(held.shape[1], -1)
    return Pieces([full], None, *full.shape)


def narrow(shard):
    return shard.shape[1] % 128 != 0


class Bank:
    def __init__(self, array, start, columns):
        self.arrays, self.start, self.columns = [array], start, columns
        self.rows = array.shape[2]


def bank_copies(bank, ref, seq, first, columns, target, sems, column):
    found = []
    for owner in range(bank.arrays[0].shape[0]):
        source = ref.at[owner, seq, :, pl.ds(bank.start + first, columns)]
        spot = target.at[pl.ds(owner * bank.rows, bank.rows), pl.ds(column, columns)]
        found.append(pltpu.make_async_copy(source, spot, sems.at[len(found)]))
    return found


def pack_kernel(count, *refs):
    *head, w_up_ref, w_down_ref = refs[:count]
    bank_ref = refs[-1]
    parts = [ref[...].T for ref in head] + [w_up_ref[...], w_down_ref[...].T]
    bank_ref[...] = jnp.concatenate(parts, 1)


def pack_bank(earlier, *weights):
    rows = weights[-2].shape[0]
    return pl.pallas_call(
        functools.partial(pack_kernel, len(weights)),
        out_shape=jax.ShapeDtypeStruct((rows, sum(weight.size for weight in weights) // rows), BF16),
        in_specs=[pl.BlockSpec(memory_space=pltpu.VMEM)] * len(weights) + [ANY_SPEC] * len(earlier),
        compiler_params=pltpu.CompilerParams(vmem_limit_bytes=VMEM_LIMIT),
        name="pack_bank",
    )(*weights, *earlier)


def unpack_kernel(chunk, sums_ref, up_ref, down_ref):
    for part in range(up_ref.shape[1] // chunk):
        start = 2 * part * chunk
        span = slice(part * chunk, (part + 1) * chunk)
        up_ref[:, span] = sums_ref[:, start : start + chunk]
        down_ref[span, :] = sums_ref[:, start + chunk : start + 2 * chunk].T


def unpack_sums(sums, units, chunk):
    rows = sums.shape[0]
    return pl.pallas_call(
        functools.partial(unpack_kernel, chunk),
        out_shape=tuple(jax.ShapeDtypeStruct(shape, F32) for shape in [(rows, units), (units, rows)]),
        compiler_params=pltpu.CompilerParams(vmem_limit_bytes=VMEM_LIMIT),
        name="unpack_sums",
    )(sums)


def weight_copies(pieces, refs, target, sems, place_ref, relative):
    if isinstance(pieces, Bank):
        copies, owners = [], pieces.arrays[0].shape[0]
        for seq in range(axis_size("seq")):
            part_sems = sems.at[pl.ds(seq * owners, owners)]
            column = pl.multiple_of((place_ref[1] ^ seq) * pieces.columns, pieces.columns)
            copies += bank_copies(pieces, refs[0], seq, 0, pieces.columns, target, part_sems, column)
        return copies
    if pieces.masks is None:
        return [pltpu.make_async_copy(refs[0], target, sems.at[0])]
    copies, rows, columns = [], pieces.rows, pieces.columns
    for ref, table in zip(refs, pieces.masks):
        for entry, (dp_mask, seq_mask) in enumerate(table):
            row = pl.multiple_of((place_ref[0] ^ dp_mask) * rows, rows)
            target_rows = target.at[pl.ds(row, rows), :]
            if target.shape[1] != columns:
                if relative:
                    column = seq_mask * columns
                else:
                    column = pl.multiple_of((place_ref[1] ^ seq_mask) * columns, columns)
                target_rows = target.at[pl.ds(row, rows), pl.ds(column, columns)]
            copies.append(pltpu.make_async_copy(ref.at[entry], target_rows, sems.at[len(copies)]))
    return copies


def copy_count(pieces):
    if isinstance(pieces, Bank):
        return axis_size("seq") * pieces.arrays[0].shape[0]
    return 1 if pieces.masks is None else sum(len(table) for table in pieces.masks)


def assemble_kernel(pieces, place_ref, *rest):
    refs, out_ref, sems = rest[:-2], rest[-2], rest[-1]
    copies = weight_copies(pieces, refs, out_ref, sems, place_ref, False)
    for copy in copies:
        copy.start()
    for copy in copies:
        copy.wait()


def assemble(pieces, place, shape):
    return pl.pallas_call(
        functools.partial(assemble_kernel, pieces),
        out_shape=jax.ShapeDtypeStruct(shape, BF16),
        in_specs=[SMEM_SPEC] + [ANY_SPEC] * len(pieces.arrays),
        out_specs=pl.BlockSpec(memory_space=pltpu.VMEM),
        scratch_shapes=[pltpu.SemaphoreType.DMA((copy_count(pieces),))],
        compiler_params=pltpu.CompilerParams(vmem_limit_bytes=VMEM_LIMIT),
        cost_estimate=pl.CostEstimate(flops=0, bytes_accessed=4 * math.prod(shape), transcendentals=0),
        name="assemble",
    )(place, *pieces.arrays)


def pick(values, index, axis):
    return lax.dynamic_index_in_dim(values, index, axis, keepdims=False)


def send_seq(held):
    total, sent = held[0], []
    for mask in range(1, held.shape[0]):
        sent.append(held[mask].astype(BF16))
        total = total + swap(sent[-1], "seq", mask).astype(F32)
    return total, sent


def send_chips(held, dtype=BF16):
    total = held[0]
    for mask in chip_masks():
        total = total + swap(held[mask // CORES].astype(dtype), "dp", mask).astype(F32)
    return total


def halve(held, axis):
    for mask in reversed(bits(axis)):
        count = held.shape[0] // 2
        held = held[:count].astype(F32) + swap(held[count:].astype(BF16), axis, mask).astype(F32)
    return held[0]


def add_cores(keep, give):
    return keep.astype(F32) + swap(give, "dp", 1).astype(F32)


def split_rows(place_ref, source_ref, rows, chip, core, by_mask):
    owner = place_ref[0] ^ (chip * CORES + core) if by_mask else chip * CORES + (place_ref[0] % CORES ^ core)
    return source_ref[pl.ds(pl.multiple_of(owner * rows, rows), rows), :]


def weight_grad_kernel(count, y_count, by_token, seqs, by_mask, place_ref, *rest):
    x_refs, y_refs, (keep_ref, give_ref, xt_ref) = rest[:count], rest[count : count + y_count], rest[-3:]
    chip = pl.program_id(0)
    rows, columns = keep_ref.shape[-2:]
    tokens, wide = x_refs[0].shape

    @pl.when(chip == 0)
    def _():
        for piece, ref in enumerate(x_refs):
            if by_token:
                xt_ref[:, piece * tokens : (piece + 1) * tokens] = ref[...].T
            else:
                xt_ref[piece * wide : (piece + 1) * wide, :] = ref[...].T

    for core, out_ref in ((0, keep_ref), (1, give_ref)):
        left = split_rows(place_ref, xt_ref, rows, chip, core, by_mask)
        result, start = 0.0, 0
        for ref in y_refs:
            part = ref[...].reshape(-1, ref.shape[-1])
            result = result + dot(left[:, start : start + part.shape[0]], part)
            start += part.shape[0]
        result = result.astype(BF16)
        for seq in range(seqs):
            out_ref[seq, 0] = result[:, seq * columns : (seq + 1) * columns]


def weight_grad(place, xs, ys, by_token, rows, seqs, by_mask, *earlier):
    chips = axis_size("dp") // CORES
    tokens, wide = xs[0].shape
    columns = ys[0].shape[-1] // seqs
    shape = (wide, len(xs) * tokens) if by_token else (len(xs) * wide, tokens)
    out = jax.ShapeDtypeStruct((seqs, chips, rows, columns), BF16)
    spec = pl.BlockSpec((seqs, 1, rows, columns), lambda i: (0, i, 0, 0))
    constant = lambda array: pl.BlockSpec(array.shape, lambda i: (0,) * array.ndim)
    return pl.pallas_call(
        functools.partial(weight_grad_kernel, len(xs), len(ys), by_token, seqs, by_mask),
        grid=(chips,),
        out_shape=(out, out),
        in_specs=[SMEM_SPEC] + [constant(array) for array in list(xs) + list(ys)] + [ANY_SPEC] * len(earlier),
        out_specs=(spec, spec),
        scratch_shapes=[pltpu.VMEM(shape, BF16)],
        compiler_params=pltpu.CompilerParams(vmem_limit_bytes=VMEM_LIMIT),
        cost_estimate=pl.CostEstimate(
            flops=2 * math.prod(shape) * columns * seqs,
            bytes_accessed=2 * math.prod(shape) + 4 * shape[0] * columns * seqs,
            transcendentals=0,
        ),
        name="weight_grad",
    )(place, *xs, *ys, *earlier)


def project_kernel(pieces, width, scale, w_ref, cos_ref, sin_ref, *rest):
    x_refs, (out_ref, x_ref) = rest[:pieces], rest[pieces:]
    half = width // 2
    for piece in range(pieces):

        @pl.when(pl.program_id(0) == piece)
        def _():
            x_ref[...] = x_refs[piece][0]

    projected = dot(x_ref[...], w_ref[...])
    cosine, sine = cos_ref[0], sin_ref[0]
    for part, factor in ((0, scale), (1, 1.0)):
        low = projected[:, part * width : part * width + half]
        high = projected[:, part * width + half : (part + 1) * width]
        out_ref[0, 0, :, part * width : part * width + half] = ((low * cosine - high * sine) * factor).astype(BF16)
        out_ref[0, 0, :, part * width + half : (part + 1) * width] = ((high * cosine + low * sine) * factor).astype(BF16)
    out_ref[0, 0, :, 2 * width :] = projected[:, 2 * width :].astype(BF16)


def project(normed, weights, cos_table, sin_table, scale):
    pieces = len(normed)
    _, frames, model = normed[0].shape
    width = weights.shape[1] // 3
    table = pl.BlockSpec((1, frames, width // 2), lambda s: (s, 0, 0))
    return pl.pallas_call(
        functools.partial(project_kernel, pieces, width, scale),
        grid=(pieces,),
        out_shape=jax.ShapeDtypeStruct((pieces, 1, frames, 3 * width), BF16),
        in_specs=[pl.BlockSpec((model, 3 * width), lambda s: (0, 0)), table, table]
        + [pl.BlockSpec((1, frames, model), lambda s: (0, 0, 0))] * pieces,
        out_specs=pl.BlockSpec((1, 1, frames, 3 * width), lambda s: (s, 0, 0, 0)),
        scratch_shapes=[pltpu.VMEM((frames, model), BF16)],
        compiler_params=pltpu.CompilerParams(vmem_limit_bytes=VMEM_LIMIT),
        cost_estimate=pl.CostEstimate(
            flops=2 * pieces * frames * model * 3 * width,
            bytes_accessed=2 * pieces * frames * (model + 3 * width),
            transcendentals=0,
        ),
        name="project",
    )(weights, cos_table, sin_table, *normed)


def spread_back_kernel(count, grad_ref, weight_ref, *rest):
    out_refs = rest[-count:]
    piece = pl.program_id(0)
    result = against(grad_ref[0, 0], weight_ref[...]).astype(BF16)
    for position, ref in enumerate(out_refs):

        @pl.when(piece == position)
        def _():
            ref[0] = result


def spread_back(grad_qkv, weights, *earlier):
    pieces, rows, frames, triple = grad_qkv.shape
    model = weights.shape[0]

    def out_spec(position):
        return pl.BlockSpec(
            (1, frames, model),
            lambda m, r: (jnp.where(m < position, 0, jnp.where(m == position, r, rows - 1)), 0, 0),
        )

    return pl.pallas_call(
        functools.partial(spread_back_kernel, pieces - 1),
        grid=(pieces - 1, rows),
        out_shape=(jax.ShapeDtypeStruct((rows, frames, model), BF16),) * (pieces - 1),
        in_specs=[
            pl.BlockSpec((1, 1, frames, triple), lambda m, r: (m + 1, r, 0, 0)),
            pl.BlockSpec(weights.shape, lambda m, r: (0, 0)),
        ]
        + [ANY_SPEC] * len(earlier),
        out_specs=tuple(out_spec(position) for position in range(pieces - 1)),
        compiler_params=pltpu.CompilerParams(vmem_limit_bytes=VMEM_LIMIT),
        cost_estimate=pl.CostEstimate(
            flops=2 * (pieces - 1) * rows * frames * triple * model,
            bytes_accessed=2 * pieces * rows * frames * (triple + model),
            transcendentals=0,
        ),
        name="spread_back",
    )(grad_qkv, weights, *earlier)


def head_lanes(shape, heads, width, split):
    lane = lax.broadcasted_iota(jnp.int32, shape, 1)
    size = width // heads
    if split:
        return (lane % (width // 2)) // (size // 2)
    return lane // size


def spread_back_kernel(count, grad_ref, weight_ref, *rest):
    out_refs = rest[-count:]
    piece = pl.program_id(0)
    result = against(grad_ref[0, 0], weight_ref[...]).astype(BF16)
    for position, ref in enumerate(out_refs):

        @pl.when(piece == position)
        def _():
            ref[0] = result


def spread_back(grad_qkv, weights, *earlier):
    pieces, rows, frames, triple = grad_qkv.shape
    model = weights.shape[0]

    def out_spec(position):
        return pl.BlockSpec(
            (1, frames, model),
            lambda m, r: (jnp.where(m < position, 0, jnp.where(m == position, r, rows - 1)), 0, 0),
        )

    return pl.pallas_call(
        functools.partial(spread_back_kernel, pieces - 1),
        grid=(pieces - 1, rows),
        out_shape=(jax.ShapeDtypeStruct((rows, frames, model), BF16),) * (pieces - 1),
        in_specs=[
            pl.BlockSpec((1, 1, frames, triple), lambda m, r: (m + 1, r, 0, 0)),
            pl.BlockSpec(weights.shape, lambda m, r: (0, 0)),
        ]
        + [ANY_SPEC] * len(earlier),
        out_specs=tuple(out_spec(position) for position in range(pieces - 1)),
        compiler_params=pltpu.CompilerParams(vmem_limit_bytes=VMEM_LIMIT),
        cost_estimate=pl.CostEstimate(
            flops=2 * (pieces - 1) * rows * frames * triple * model,
            bytes_accessed=2 * pieces * rows * frames * (triple + model),
            transcendentals=0,
        ),
        name="spread_back",
    )(grad_qkv, weights, *earlier)


def head_lanes(shape, heads, width, split):
    lane = lax.broadcasted_iota(jnp.int32, shape, 1)
    size = width // heads
    if split:
        return (lane % (width // 2)) // (size // 2)
    return lane // size


def column_of(row, lanes):
    return jnp.broadcast_to(row, (128, row.shape[1])).T[:, :lanes]


def attend_kernel(heads, width, qkv_ref, seg_ref, *rest):
    pieces, _, frames, _ = qkv_ref.shape
    out_refs, (lse_ref, vt_ref, ot_ref, seg_col_ref) = rest[:pieces], rest[pieces:]
    length = pieces * frames
    step = pl.program_id(1)
    size = width // heads
    keys = qkv_ref[:, 0, :, width : 2 * width].reshape(length, width)

    @pl.when(step == 0)
    def _():
        vt_ref[...] = qkv_ref[:, 0, :, 2 * width :].reshape(length, width).T
        for piece in range(pieces):
            seg_col_ref[piece * frames : (piece + 1) * frames, :] = column_of(seg_ref[0, piece : piece + 1, :], 128)

    queries = qkv_ref[step, 0, :, :width]
    owner = head_lanes((frames, width), heads, width, True)
    allowed = seg_col_ref[:, :1] == seg_ref[0, pl.ds(step, 1), :]
    for head in range(heads):
        masked = jnp.where(owner == head, queries, jnp.zeros_like(queries))
        scores = jnp.where(allowed, against(keys, masked), MASKED)
        highest = jnp.max(scores, 0, keepdims=True)
        raised = jnp.exp(scores - highest)
        total = jnp.sum(raised, 0, keepdims=True)
        lse_ref[0, 0, head : head + 1, :] = highest + jnp.log(total)
        result = dot(vt_ref[head * size : (head + 1) * size, :], raised.astype(BF16))
        ot_ref[head * size : (head + 1) * size, :] = result / total
    result = ot_ref[...].T.astype(BF16)
    for piece in range(pieces):

        @pl.when(step == piece)
        def _():
            out_refs[piece][0] = result


def attend(qkv, seg, row, heads):
    pieces, rows, frames, triple = qkv.shape
    width = triple // 3
    length = pieces * frames
    results = pl.pallas_call(
        functools.partial(attend_kernel, heads, width),
        grid=(rows, pieces),
        out_shape=(jax.ShapeDtypeStruct((rows, frames, width), BF16),) * pieces
        + (jax.ShapeDtypeStruct((rows, pieces, heads, frames), F32),),
        in_specs=[
            pl.BlockSpec((pieces, 1, frames, triple), lambda r, s: (0, r, 0, 0)),
            pl.BlockSpec((1, pieces, frames), lambda r, s: (row, 0, 0)),
        ],
        out_specs=(pl.BlockSpec((1, frames, width), lambda r, s: (r, 0, 0)),) * pieces
        + (pl.BlockSpec((1, 1, heads, frames), lambda r, s: (r, s, 0, 0)),),
        scratch_shapes=[
            pltpu.VMEM((width, length), BF16),
            pltpu.VMEM((width, frames), F32),
            pltpu.VMEM((length, 128), F32),
        ],
        compiler_params=pltpu.CompilerParams(vmem_limit_bytes=VMEM_LIMIT),
        cost_estimate=pl.CostEstimate(
            flops=4 * rows * length * length * 256 * heads,
            bytes_accessed=8 * rows * length * width,
            transcendentals=rows * heads * length * length,
        ),
        name="attend",
    )(qkv, seg)
    return results[:pieces], results[pieces]


def attend_back_kernel(heads, width, scale, qkv_ref, seg_ref, lse_ref, cos_ref, sin_ref, *rest):
    pieces, _, frames, _ = qkv_ref.shape
    out_refs, grad_refs = rest[:pieces], rest[pieces : 2 * pieces]
    result_ref, kt_ref, dk_ref, dv_ref, dqt_ref, seg_col_ref, out_ref, grad_ref = rest[-8:]
    length = pieces * frames
    step = pl.program_id(1)
    size, half = width // heads, width // 2
    keys = qkv_ref[:, 0, :, width : 2 * width].reshape(length, width)
    values = qkv_ref[:, 0, :, 2 * width :].reshape(length, width)

    @pl.when(step == 0)
    def _():
        kt_ref[...] = keys.T
        dk_ref[...] = jnp.zeros_like(dk_ref)
        dv_ref[...] = jnp.zeros_like(dv_ref)
        for piece in range(pieces):
            seg_col_ref[piece * frames : (piece + 1) * frames, :] = column_of(seg_ref[0, piece : piece + 1, :], 128)
            out_ref[piece] = out_refs[piece][0]
            grad_ref[piece] = grad_refs[piece][0]

    queries = qkv_ref[step, 0, :, :width]
    grad = grad_ref[step]
    query_owner = head_lanes((frames, width), heads, width, True)
    value_owner = head_lanes((frames, width), heads, width, False)
    allowed = seg_col_ref[:, :1] == seg_ref[0, pl.ds(step, 1), :]
    product = grad.astype(F32) * out_ref[step].astype(F32)
    picker = lax.broadcasted_iota(jnp.int32, (8, width), 1) // size == lax.broadcasted_iota(jnp.int32, (8, width), 0)
    inner = lax.dot_general(
        picker.astype(F32), product, NT, precision=lax.Precision.HIGHEST, preferred_element_type=F32
    )
    for head in range(heads):
        masked = jnp.where(query_owner == head, queries, jnp.zeros_like(queries))
        masked_grad = jnp.where(value_owner == head, grad, jnp.zeros_like(grad))
        scores = against(keys, masked)
        weights = jnp.where(allowed, jnp.exp(scores - lse_ref[0, 0, head : head + 1, :]), 0.0)
        grad_weights = against(values, masked_grad)
        grad_scores = (weights * (grad_weights - inner[head : head + 1, :])).astype(BF16)
        dv_ref[...] += dot(weights.astype(BF16), masked_grad)
        dk_ref[...] += dot(grad_scores, masked)
        low, high = head * size // 2, half + head * size // 2
        head_keys = jnp.concatenate([kt_ref[low : low + size // 2, :], kt_ref[high : high + size // 2, :]], 0)
        part = dot(head_keys, grad_scores)
        dqt_ref[low : low + size // 2, :] = part[: size // 2]
        dqt_ref[high : high + size // 2, :] = part[size // 2 :]

    def unrotate(values, cosine, sine):
        low, high = values[:, :half], values[:, half:]
        return (low * cosine + high * sine).astype(BF16), (high * cosine - low * sine).astype(BF16)

    low, high = unrotate(dqt_ref[...].T * scale, cos_ref[step], sin_ref[step])
    result_ref[step, 0, :, :half] = low
    result_ref[step, 0, :, half:width] = high

    @pl.when(step == pieces - 1)
    def _():
        for piece in range(pieces):
            span = slice(piece * frames, (piece + 1) * frames)
            low, high = unrotate(dk_ref[span, :], cos_ref[piece], sin_ref[piece])
            result_ref[piece, 0, :, width : width + half] = low
            result_ref[piece, 0, :, width + half : 2 * width] = high
            result_ref[piece, 0, :, 2 * width :] = dv_ref[span, :].astype(BF16)


def attend_back(qkv, seg, row, lse, cos_table, sin_table, outs, grads, heads, scale, earlier):
    pieces, rows, frames, triple = qkv.shape
    width = triple // 3
    length = pieces * frames
    whole = pl.BlockSpec((pieces, 1, frames, triple), lambda r, s: (0, r, 0, 0))
    table = pl.BlockSpec((pieces, frames, width // 2), lambda r, s: (0, 0, 0))
    block = pl.BlockSpec((1, frames, width), lambda r, s: (r, 0, 0))
    return pl.pallas_call(
        functools.partial(attend_back_kernel, heads, width, scale),
        grid=(rows, pieces),
        out_shape=jax.ShapeDtypeStruct(qkv.shape, BF16),
        in_specs=[
            whole,
            pl.BlockSpec((1, pieces, frames), lambda r, s: (row, 0, 0)),
            pl.BlockSpec((1, 1, heads, frames), lambda r, s: (r, s, 0, 0)),
            table,
            table,
        ]
        + [block] * (2 * pieces)
        + [ANY_SPEC] * len(earlier),
        out_specs=whole,
        scratch_shapes=[
            pltpu.VMEM((width, length), BF16),
            pltpu.VMEM((length, width), F32),
            pltpu.VMEM((length, width), F32),
            pltpu.VMEM((width, frames), F32),
            pltpu.VMEM((length, 128), F32),
            pltpu.VMEM((pieces, frames, width), BF16),
            pltpu.VMEM((pieces, frames, width), BF16),
        ],
        compiler_params=pltpu.CompilerParams(vmem_limit_bytes=VMEM_LIMIT),
        cost_estimate=pl.CostEstimate(
            flops=10 * rows * length * length * 256 * heads,
            bytes_accessed=16 * rows * length * width,
            transcendentals=rows * heads * length * length,
        ),
        name="attend_back",
    )(qkv, seg, lse, cos_table, sin_table, *outs, *grads, *earlier)


def mlp_kernel(bank, chunk, place_ref, normed_ref, grad_ref, bank_ref, *rest):
    fed_ref, gn_ref, grads_ref, nt_ref, gt_ref, weight_ref, result_ref, sems = rest
    step, rows = pl.program_id(0), bank.rows
    units = bank.columns // 2
    per_place = units // chunk
    half = bank.arrays[0].shape[0]

    def copies(block, slot):
        start = (block % per_place) * chunk
        target, found = weight_ref.at[slot], []
        for which in range(2):
            found += bank_copies(
                bank, bank_ref, block // per_place, which * units + start, chunk, target,
                sems.at[slot, pl.ds(which * half, half)], which * chunk,
            )
        return found

    @pl.when(step == 0)
    def _():
        for copy in copies(0, 0):
            copy.start()
        nt_ref[...] = normed_ref[...].T
        gt_ref[...] = grad_ref[...].T
        fed_ref[...] = jnp.zeros_like(fed_ref)
        gn_ref[...] = jnp.zeros_like(gn_ref)

    for block in range(1, axis_size("seq") * per_place):

        @pl.when(step + 1 == block)
        def _():
            for copy in copies(block, block % 2):
                copy.start()

    slot = step % 2
    for copy in copies(0, slot):
        copy.wait()
    up, down = weight_ref[slot, :, :chunk], weight_ref[slot, :, chunk:]
    before = dot(normed_ref[...], up)
    square = before * before
    factor = math.sqrt(2.0 / math.pi)
    bent = jnp.tanh(factor * (before + 0.044715 * (square * before)))
    activated = (0.5 * before * (1.0 + bent)).astype(BF16)
    slope = 0.5 * (1.0 + bent) + 0.5 * before * (1.0 - bent * bent) * (factor * (1.0 + 3 * 0.044715 * square))
    grad_before = (dot(grad_ref[...], down) * slope).astype(BF16)
    fed_ref[...] += against(activated, down)
    gn_ref[...] += against(grad_before, up)
    result_ref[:, :chunk] = dot(nt_ref[...], grad_before).astype(BF16)
    result_ref[:, chunk:] = dot(gt_ref[...], activated).astype(BF16)
    for owner in range(grads_ref.shape[0]):
        grads_ref[owner, 0] = result_ref[owner * rows : (owner + 1) * rows, :]


def mlp(place, normed, grad, bank):
    tokens, model = normed.shape
    seqs, owners = axis_size("seq"), axis_size("dp")
    units = bank.columns // 2
    chunk = min(1024, units)
    per_place = units // chunk
    whole = pl.BlockSpec((tokens, model), lambda i: (0, 0))
    hidden = seqs * units
    return pl.pallas_call(
        functools.partial(mlp_kernel, bank, chunk),
        grid=(seqs * per_place,),
        out_shape=(jax.ShapeDtypeStruct((tokens, model), F32),) * 2
        + (jax.ShapeDtypeStruct((owners, seqs, bank.rows, 2 * units), BF16),),
        in_specs=[SMEM_SPEC, whole, whole, ANY_SPEC],
        out_specs=(
            whole,
            whole,
            pl.BlockSpec((owners, 1, bank.rows, 2 * chunk), lambda i: (0, i // per_place, 0, i % per_place)),
        ),
        scratch_shapes=[
            pltpu.VMEM((model, tokens), BF16),
            pltpu.VMEM((model, tokens), BF16),
            pltpu.VMEM((2, model, 2 * chunk), BF16),
            pltpu.VMEM((model, 2 * chunk), BF16),
            pltpu.SemaphoreType.DMA((2, 2 * owners)),
        ],
        compiler_params=pltpu.CompilerParams(vmem_limit_bytes=VMEM_LIMIT),
        cost_estimate=pl.CostEstimate(
            flops=12 * tokens * model * hidden,
            bytes_accessed=8 * model * hidden + 12 * tokens * model,
            transcendentals=tokens * hidden,
        ),
        name="mlp",
    )(place, normed, grad, *bank.arrays)


def standardize(values):
    centre = values - jnp.mean(values, -1, keepdims=True)
    inverse = lax.rsqrt(jnp.mean(centre * centre, -1, keepdims=True) + EPSILON)
    return centre * inverse, inverse


def standardize_back(grad, standard, inverse):
    return inverse * (
        grad - jnp.mean(grad, -1, keepdims=True) - standard * jnp.mean(grad * standard, -1, keepdims=True)
    )


def utterance_of(seg_ref):
    return column_of(seg_ref[0], 1)


def by_frame(owner, mod_ref, part):
    count = mod_ref.shape[1]
    result = mod_ref[0, count - 1, part : part + 1, :]
    for position in range(count - 2, -1, -1):
        result = jnp.where(owner == float(position), mod_ref[0, position, part : part + 1, :], result)
    return result


def add_up(owner, values, out_ref, part, count):
    for position in range(count):
        out_ref[0, part, position : position + 1, :] = jnp.sum(
            jnp.where(owner == float(position), values, 0.0), 0, keepdims=True
        )


def start_weight(pieces, refs, target, sems, place_ref, relative):
    copies = weight_copies(pieces, refs, target, sems, place_ref, relative)
    for copy in copies:
        copy.start()
    return copies


def wait_all(copies):
    for copy in copies:
        copy.wait()


def row_call(kernel, name, place, row, by_row, fixed, pieces, weight_shape, outs, held, flops, earlier=()):
    def row_spec(shape):
        lead = 0 if len(shape) == 4 and shape[1] == 1 else row if shape[0] > 1 else 0
        return pl.BlockSpec((1,) + tuple(shape[1:]), lambda i: (lead,) + (0,) * (len(shape) - 1))

    fixed_specs = [pl.BlockSpec(array.shape, lambda i, n=array.ndim: (0,) * n) for array in fixed]
    size = sum(array.size * array.dtype.itemsize for array in by_row) + 2 * math.prod(weight_shape)
    first = len(place) + len(by_row) + len(fixed) + len(pieces.arrays)
    kept = [position for position, out in enumerate(outs) if held and out.shape[0] > 1]
    held = [held[position] for position in kept]
    aliases = {first + number: position for number, position in enumerate(kept)}
    return pl.pallas_call(
        kernel,
        grid=(1,),
        out_shape=tuple(outs),
        in_specs=[SMEM_SPEC] * len(place)
        + [row_spec(array.shape) for array in by_row]
        + fixed_specs
        + [ANY_SPEC] * (len(pieces.arrays) + len(held) + len(earlier)),
        out_specs=tuple(row_spec(out.shape) for out in outs),
        input_output_aliases=aliases,
        scratch_shapes=[pltpu.VMEM(weight_shape, BF16), pltpu.SemaphoreType.DMA((copy_count(pieces),))],
        compiler_params=pltpu.CompilerParams(vmem_limit_bytes=VMEM_LIMIT),
        cost_estimate=pl.CostEstimate(flops=flops, bytes_accessed=size, transcendentals=0),
        name=name,
    )(*place, *by_row, *fixed, *pieces.arrays, *held, *earlier)


def enter_kernel(pieces, row, place_ref, coef_ref, frames_ref, skip_ref, cond_ref, seg_ref, mod_ref, *rest):
    refs, (hidden_ref, normed_ref, weight_ref, sems) = rest[: len(pieces.arrays)], rest[-4:]
    copies = start_weight(pieces, refs, weight_ref, sems, place_ref, False)
    model = frames_ref.shape[2]
    owner = utterance_of(seg_ref)
    count = mod_ref.shape[1]
    factor = coef_ref[row, count - 1]
    for position in range(count - 2, -1, -1):
        factor = jnp.where(owner == float(position), coef_ref[row, position], factor)
    wait_all(copies)
    hidden = dot(frames_ref[0], weight_ref[:model, :]) + dot(skip_ref[0], weight_ref[model:, :])
    hidden = hidden + factor * cond_ref[0].astype(F32)
    hidden_ref[0] = hidden
    standard, _ = standardize(hidden)
    normed_ref[0] = (standard * (1.0 + by_frame(owner, mod_ref, 1)) + by_frame(owner, mod_ref, 0)).astype(BF16)


def branch_kernel(pieces, count, place_ref, *rest):
    blocks, (hidden_ref, cot_ref, seg_ref, mod_ref) = rest[:count], rest[count : count + 4]
    refs = rest[count + 4 : count + 4 + len(pieces.arrays)]
    attn_ref, branch_ref, middle_ref, normed_ref, grad_ref, weight_ref, sems = rest[-7:]
    copies = start_weight(pieces, refs, weight_ref, sems, place_ref, True)
    owner = utterance_of(seg_ref)
    attn = jnp.concatenate([block[0] for block in blocks], -1)
    attn_ref[0] = attn
    wait_all(copies)
    branch = against(attn, weight_ref[...])
    branch_ref[0] = branch
    middle = hidden_ref[0] + by_frame(owner, mod_ref, 2) * branch
    middle_ref[0] = middle
    standard, _ = standardize(middle)
    normed_ref[0] = (standard * (1.0 + by_frame(owner, mod_ref, 4)) + by_frame(owner, mod_ref, 3)).astype(BF16)
    grad_ref[0] = (by_frame(owner, mod_ref, 5) * cot_ref[0].astype(F32)).astype(BF16)


def middle_back_kernel(pieces, seqs, place_ref, middle_ref, fed_ref, gn_ref, cot_ref, branch_ref, seg_ref, mod_ref, *rest):
    refs = rest[: len(pieces.arrays)]
    output_ref, grad_ref, grad_branch_ref, sums_ref = rest[-6 - seqs : -2 - seqs]
    block_refs, (weight_ref, sems) = rest[-2 - seqs : -2], rest[-2:]
    copies = start_weight(pieces, refs, weight_ref, sems, place_ref, True)
    owner, count = utterance_of(seg_ref), mod_ref.shape[1]
    middle, fed, grad_norm, grad_out = middle_ref[0], fed_ref[0], gn_ref[0], cot_ref[0].astype(F32)
    output_ref[0] = (middle + by_frame(owner, mod_ref, 5) * fed).astype(BF16)
    standard, inverse = standardize(middle)
    grad_middle = grad_out + standardize_back(grad_norm * (1.0 + by_frame(owner, mod_ref, 4)), standard, inverse)
    grad_ref[0] = grad_middle
    grad_branch = (by_frame(owner, mod_ref, 2) * grad_middle).astype(BF16)
    grad_branch_ref[0] = grad_branch
    wait_all(copies)
    grad_attn = dot(grad_branch, weight_ref[...]).astype(BF16)
    width = grad_attn.shape[1] // seqs
    for seq in range(seqs):
        block_refs[seq][0] = grad_attn[:, seq * width : (seq + 1) * width]
    add_up(owner, grad_middle * branch_ref[0], sums_ref, 0, count)
    add_up(owner, grad_norm, sums_ref, 1, count)
    add_up(owner, grad_norm * standard, sums_ref, 2, count)
    add_up(owner, grad_out * fed, sums_ref, 3, count)


def leave_kernel(pieces, seqs, place_ref, hidden_ref, grad_middle_ref, own_ref, *rest):
    got = rest[: seqs - 1]
    seg_ref, mod_ref, qkv_ref = rest[seqs - 1 : seqs + 2]
    refs = rest[seqs + 2 : seqs + 2 + len(pieces.arrays)]
    columns_ref, frames_ref, skip_ref, sums_ref, weight_ref, sems = rest[-6:]
    copies = start_weight(pieces, refs, weight_ref, sems, place_ref, False)
    owner, count = utterance_of(seg_ref), mod_ref.shape[1]
    grad_norm = against(own_ref[0, 0], qkv_ref[...])
    for ref in got:
        grad_norm = grad_norm + ref[0].astype(F32)
    standard, inverse = standardize(hidden_ref[0])
    grad = standardize_back(grad_norm * (1.0 + by_frame(owner, mod_ref, 1)), standard, inverse)
    grad_hidden = (grad_middle_ref[0] + grad).astype(BF16)
    model = grad_hidden.shape[1]
    wait_all(copies)
    frames_ref[0] = against(grad_hidden, weight_ref[:model, :]).astype(BF16)
    skip_ref[0] = against(grad_hidden, weight_ref[model:, :]).astype(BF16)
    add_up(owner, grad_norm, sums_ref, 0, count)
    add_up(owner, grad_norm * standard, sums_ref, 1, count)
    width = model // seqs
    turned = grad_hidden.astype(F32)
    bit = 1
    while bit < seqs:
        parts = [turned[:, (s ^ bit) * width : ((s ^ bit) + 1) * width] for s in range(seqs)]
        turned = jnp.where((place_ref[1] // bit) % 2 == 1, jnp.concatenate(parts, -1), turned)
        bit *= 2
    columns_ref[0] = turned.astype(BF16)


def time_embed(flow_values, model_width):
    half_dim = model_width // 2
    frequency = jnp.exp(jnp.arange(half_dim, dtype=F32) * (-math.log(10000.0) / half_dim))
    angles = 1000.0 * flow_values[..., None] * frequency
    return jnp.concatenate([jnp.sin(angles), jnp.cos(angles)], -1)


def body(
    frames, skip_in, cond, seg_ids, drop_flags, flow_times, w_skip, w_qkv, w_out, w_up, w_down, w_mod, cotangent
):
    row_count, frame_count, model = frames.shape
    seq_size, dp_size = axis_size("seq"), axis_size("dp")
    chips = dp_size // CORES
    dp, seq = lax.axis_index(AXES["dp"]), lax.axis_index(AXES["seq"])
    place = jnp.stack([dp, seq]).astype(jnp.int32)
    head_dim = model // HEADS
    heads = HEADS // seq_size
    width = heads * head_dim
    half = head_dim // 2
    scale = head_dim ** (-0.5)
    tokens = row_count * frame_count
    segs = drop_flags.shape[1]
    frame_shape = (row_count, frame_count, model)
    partners = range(1, seq_size)
    fast, slow = seq_halves()
    rows = w_up.shape[0]
    shape_of = jax.ShapeDtypeStruct

    by_head = w_qkv.reshape(w_qkv.shape[0], heads, 3, 2, half)
    qkv_shard = jnp.concatenate(
        [
            by_head[:, :, 0].swapaxes(1, 2).reshape(-1, width),
            by_head[:, :, 1].swapaxes(1, 2).reshape(-1, width),
            by_head[:, :, 2].reshape(-1, width),
        ],
        1,
    )
    skip_parts = pack(gather_over(start_gather(w_skip), "dp", chip_masks()))

    skip_near = skip_parts.arrays[0]

    small = jnp.concatenate([flow_times, drop_flags.astype(F32)], 1)
    small = gather_steps(small, [("dp", chip_masks())])
    mod_rows, mod_columns = w_mod.shape
    mod_pair = swap(w_mod, "dp", 1)
    utterances = row_count * segs

    def activity_of(values, owner):
        result = jax.nn.silu(time_embed(values, model)).astype(BF16).reshape(-1, model)
        return lax.dynamic_slice_in_dim(result, owner * mod_rows, mod_rows, 1)

    modulation = dot(activity_of(small[..., :segs], dp), w_mod)
    modulation = modulation + dot(activity_of(small[..., :segs], dp ^ 1), mod_pair)
    modulation = modulation.reshape(chips, utterances, mod_columns)
    for mask in reversed(bits("dp")):
        count = modulation.shape[0] // 2
        modulation = modulation[:count] + swap(modulation[count:], "dp", mask)
    modulation = modulation[0]

    small = jnp.stack([small, swap(small, "dp", 1)])
    dropped = jnp.sum(small[..., segs:])
    slots = float(row_count * segs * dp_size)
    cond_scale = slots / jnp.maximum(slots - dropped, 1.0)
    coefficients = (1.0 - drop_flags.astype(F32)) * cond_scale

    if narrow(w_skip):
        skip_parts = whole_columns(w_skip, place, False)
        arrived = skip_parts.arrays[0]
    else:
        skip_parts = gather_over(skip_parts, "seq", partners)
        arrived = skip_parts.arrays[-1]
        skip_parts = gather_over(skip_parts, "dp", [1])

    extra = -(-tokens // mod_columns)
    numbers = jnp.pad(seg_ids.astype(F32).reshape(-1), (0, extra * mod_columns - tokens)).reshape(extra, mod_columns)
    own_mod = jnp.concatenate([modulation, numbers])
    all_mod = jnp.stack([own_mod] + [swap(own_mod, "seq", mask) for mask in partners])
    segments = all_mod[:, utterances:].reshape(seq_size, -1)[:, :tokens].reshape(seq_size, row_count, frame_count)
    segments = segments.swapaxes(0, 1)
    modulation = jnp.take(all_mod[:, :utterances], jnp.arange(seq_size) ^ seq, axis=0)
    modulation = modulation.swapaxes(0, 1).reshape(row_count, segs, 6, model)
    seg_here = segments[:, :1]

    qkv_parts = start_gather(qkv_shard)
    for mask in bits("dp"):
        qkv_parts = pack(gather_over(qkv_parts, "dp", [mask]))
    qkv_full = assemble(gather_over(qkv_parts, "dp", [1]), place, (dp_size * rows, 3 * width))

    units = w_up.shape[1]
    bank = pack_bank([arrived, all_mod, qkv_parts.arrays[0]], w_up, w_down)
    bank = lax.all_gather(bank, AXES["all"], axis=0)
    bank = Bank(bank.reshape((dp_size, seq_size) + bank.shape[1:]), 0, 2 * units)

    row_range = range(row_count)
    one_row = (1,) + frame_shape[1:]
    entered, normed = None, []
    for row in row_range:
        entered = row_call(
            functools.partial(enter_kernel, skip_parts, row),
            "enter",
            [place, coefficients],
            row,
            [frames, skip_in, cond, seg_here, modulation],
            [],
            skip_parts,
            (2 * model, model),
            [shape_of(frame_shape, F32), shape_of(one_row, BF16)],
            entered,
            4 * frame_count * model * model,
        )
        normed.append(entered[1])
    hidden = entered[0]

    positions = (jnp.arange(seq_size) ^ seq)[:, None] * frame_count + jnp.arange(frame_count)
    frequency = jnp.exp((jnp.arange(width // 2) % half).astype(F32) * (-2.0 * math.log(10000.0) / head_dim))
    angles = positions.astype(F32)[..., None] * frequency
    cos_table, sin_table = jnp.cos(angles), jnp.sin(angles)

    pieces = [[normed[row]] + [swap(normed[row], "seq", mask) for mask in partners] for row in row_range]
    if narrow(w_out.T):
        out_parts = whole_columns(w_out.T, place, True)
    else:
        out_parts = pack(gather_over(start_gather(after(w_out.T, pieces[0][-1])), "dp", chip_masks()))
        out_parts = gather_over(gather_over(out_parts, "seq", partners), "dp", [1])
    qkv, attended, lse, branched = [], [], [], None
    for row in row_range:
        qkv.append(project(pieces[row], qkv_full, cos_table, sin_table, scale))
        result = attend(qkv[row], segments, row, heads)
        attended.append(result[0])
        lse.append(result[1])
    for row in row_range:
        blocks = [attended[row][0]] + [swap(attended[row][mask], "seq", mask) for mask in partners]
        branched = row_call(
            functools.partial(branch_kernel, out_parts, seq_size),
            "branch",
            [place],
            row,
            blocks + [hidden, cotangent, seg_here, modulation],
            [],
            out_parts,
            (model, model),
            [shape_of(frame_shape, dtype) for dtype in (BF16, F32, F32, BF16, BF16)],
            branched,
            2 * frame_count * model * model,
        )
    attn, branch, middle, normed_two, grad_fed = branched
    fed, grad_norm_two, grad_bank = mlp(
        place, normed_two.reshape(tokens, model), grad_fed.reshape(tokens, model), bank
    )
    sum_bank = lax.psum_scatter(grad_bank, AXES["dp"], scatter_dimension=0, tiled=True)[0]
    fed, grad_norm_two = fed.reshape(frame_shape), grad_norm_two.reshape(frame_shape)
    returned, grad_heads, sums_two = None, [], []
    for row in row_range:
        returned = row_call(
            functools.partial(middle_back_kernel, out_parts, seq_size),
            "middle_back",
            [place],
            row,
            [middle, fed, grad_norm_two, cotangent, branch, seg_here, modulation],
            [],
            out_parts,
            (model, model),
            [
                shape_of(frame_shape, BF16),
                shape_of(frame_shape, F32),
                shape_of(frame_shape, BF16),
                shape_of((1, 4, 8, model), F32),
            ]
            + [shape_of((1, frame_count, width), BF16)] * seq_size,
            returned,
            2 * frame_count * model * model,
        )
        sums_two.append(returned[3])
        grad_heads.append([returned[4]] + [swap(returned[4 + mask], "seq", mask) for mask in partners])
    output, grad_middle, grad_branch = returned[:3]
    keep_out, give_out = weight_grad(
        place, [grad_branch.reshape(tokens, model)], [attn.reshape(tokens, model)], True, rows, seq_size, False
    )
    sum_out, _ = send_seq(add_cores(keep_out, give_out))

    grad_qkv, got, partials = [], [], []
    for row in row_range:
        grad_qkv.append(
            attend_back(
                qkv[row], segments, row, lse[row], cos_table, sin_table, attended[row], grad_heads[row], heads, scale,
                partials,
            )
        )
        earlier = [sum_out] if row == row_count - 1 else []
        partials = spread_back(grad_qkv[row], qkv_full, *earlier)
        got.append([swap(partial, "seq", mask) for mask, partial in zip(partners, partials)])
    keep_qkv, give_qkv = weight_grad(
        place,
        [piece.reshape(frame_count, model) for row_pieces in pieces for piece in row_pieces],
        grad_qkv,
        True,
        rows,
        1,
        False,
        got[0][-1],
    )
    sum_pair = jnp.concatenate([sum_out, add_cores(keep_qkv, give_qkv)[0]], -1).astype(BF16)
    sum_pair = after(sum_pair, sum_bank)
    sum_pair = after(lax.psum_scatter(sum_pair, "chip", scatter_dimension=0, tiled=True)[0]).astype(F32)

    left, sums_one = None, []
    for row in row_range:
        left = row_call(
            functools.partial(leave_kernel, skip_parts, seq_size),
            "leave",
            [place],
            row,
            [hidden, grad_middle, grad_qkv[row]] + got[row] + [seg_here, modulation],
            [qkv_full],
            skip_parts,
            (2 * model, model),
            [shape_of(frame_shape, BF16)] * 3 + [shape_of((1, 2, 8, model), F32)],
            left,
            6 * frame_count * model * model,
            [keep_qkv] if row == 0 else [],
        )
        sums_one.append(left[3])
    grad_columns, grad_frames, grad_skip = left[:3]
    sums_one, sums_two = jnp.concatenate(sums_one), jnp.concatenate(sums_two)
    grad_modulation = jnp.concatenate([sums_one, sums_two], 1)[:, :, :segs]
    grad_modulation = grad_modulation.swapaxes(1, 2).reshape(utterances, 6 * model)
    own = lax.dynamic_slice_in_dim(grad_modulation, seq * mod_columns, mod_columns, 1)
    for mask in partners:
        own = own + swap(
            lax.dynamic_slice_in_dim(grad_modulation, (seq ^ mask) * mod_columns, mod_columns, 1), "seq", mask
        )
    keep_skip, give_skip = weight_grad(
        place,
        [frames.reshape(tokens, model), skip_in.reshape(tokens, model)],
        [grad_columns.reshape(tokens, model)],
        False,
        w_skip.shape[0],
        seq_size,
        True,
        own,
    )
    sum_skip, _ = send_seq(add_cores(keep_skip, give_skip))

    wide = pick(sum_bank, seq, 0).astype(F32)
    for mask in partners:
        wide = wide + swap(pick(sum_bank, seq ^ mask, 0), "seq", mask).astype(F32)
    sum_up, sum_down = unpack_sums(wide, units, min(1024, units))
    skip_shard = send_chips(sum_skip)
    sum_out, sum_qkv = sum_pair[:, :width].T, sum_pair[:, width:]
    sum_qkv = jnp.stack(
        [
            sum_qkv[:, :width].reshape(rows, 2, heads, half).swapaxes(1, 2).reshape(rows, heads, head_dim),
            sum_qkv[:, width : 2 * width].reshape(rows, 2, heads, half).swapaxes(1, 2).reshape(rows, heads, head_dim),
            sum_qkv[:, 2 * width :].reshape(rows, heads, head_dim),
        ],
        2,
    ).reshape(rows, 3 * width)

    own = gather_steps(own, [("dp", chip_masks()), ("dp", [1])]).reshape(dp_size * utterances, mod_columns)
    activity = activity_of(small[..., :segs], dp)
    sum_mod = jnp.dot(activity.astype(F32).T, own, precision=lax.Precision.HIGHEST)
    return (
        output,
        grad_frames,
        grad_skip,
        skip_shard,
        sum_qkv,
        sum_out,
        sum_up,
        sum_down,
        sum_mod,
    )


def solution(mesh):
    chips, seqs = mesh.shape["dp"] // CORES, mesh.shape["seq"]
    fast = 1
    while fast * fast < seqs:
        fast *= 2
    cut = Mesh(mesh.devices.reshape(chips, CORES, seqs // fast, fast), ("chip", "core", "slow", "fast"))
    dp, seq = AXES["dp"], AXES["seq"]
    tokens, rows, both, turned = P(dp, seq, None), P(dp, None), P(dp, seq), P(seq, dp)
    in_specs = (tokens, tokens, tokens, both, rows, rows, both, both, turned, both, turned, both, tokens)
    out_specs = (tokens, tokens, tokens, both, both, turned, both, turned, both)
    return jax.shard_map(body, mesh=cut, in_specs=in_specs, out_specs=out_specs, check_vma=False)
```
